256 devices in a mesh: section: 4 (over z_lo), rep: 8 (over z_hi, x), tp: 8 (over y, core).
Axes of the slice: x: 4, y: 4, z: 8 (z_hi: 2, z_lo: 4; z = z_hi * 4 + z_lo), core: 2. Of those that a mesh axis runs over, the one named last changes fastest.
Arguments:
- prefill_query: bfloat16 [256, 256, 4096], P(('section', 'rep'), None, 'tp'), may hold values from -1.0546875 to 1.0546875
- prefill_key: bfloat16 [256, 256, 4096], P(('section', 'rep'), None, 'tp'), may hold values from -1.0546875 to 1.0546875
- prefill_value: bfloat16 [256, 256, 4096], P(('section', 'rep'), None, 'tp'), may hold values from -6 to 6
- prefill_gate: float32 [256, 256, 32], P(('section', 'rep'), None, 'tp'), may hold values from 0.45 to 1
- lengths: int32 [256], replicated, may hold values from 1 to 256, 40960 in all
- decode_group: int32 [256], replicated, may hold values from 0 to 31, as said below
- cache_keys: bfloat16 [256, 256, 1024], P(('section', 'rep'), None, 'tp'), may hold values from -6 to 6
- cache_values: bfloat16 [256, 256, 1024], P(('section', 'rep'), None, 'tp'), may hold values from -6 to 6
- out_weight: bfloat16 [4096, 6144], P('tp'), may hold values from -0.09375 to 0.09375
- norm_gain: float32 [6144], replicated, may hold values from 0.25 to 1.75
- step_input: bfloat16 [4, 256, 6144], P(None, ('section', 'rep')), may hold values from -3 to 3
- step_query: bfloat16 [4, 256, 4096], P(None, ('section', 'rep'), 'tp'), may hold values from -1.0546875 to 1.0546875
- step_key: bfloat16 [4, 256, 4096], P(None, ('section', 'rep'), 'tp'), may hold values from -1.0546875 to 1.0546875
- step_value: bfloat16 [4, 256, 4096], P(None, ('section', 'rep'), 'tp'), may hold values from -6 to 6
- step_gate: float32 [4, 256, 32], P(None, ('section', 'rep'), 'tp'), may hold values from 0.5 to 1
- soft_query: bfloat16 [4, 256, 8192], P(None, ('section', 'rep'), 'tp'), may hold values from -50 to 50
- soft_new_key: bfloat16 [4, 256, 1024], P(None, ('section', 'rep'), 'tp'), may hold values from -4 to 4
- soft_new_value: bfloat16 [4, 256, 1024], P(None, ('section', 'rep'), 'tp'), may hold values from -6 to 6
Outputs:
- prefill_out: bfloat16 [256, 256, 4096], P(('section', 'rep'), None, 'tp')
- decode_out: bfloat16 [4, 256, 6144], P(None, ('section', 'rep'))
- soft_out: bfloat16 [4, 256, 8192], P(None, ('section', 'rep'), 'tp')
The draws below stay inside these ranges and needn't reach their ends.
Inputs may be any that keep to these rules, and one draw needn't show every extreme that they name: `decode_group`: request group g holds requests g * 8 to g * 8 + 7; a group g has section index g // 8 and rep index g % 8. Every group receives exactly 8 requests. The requests of one group name each rep index exactly 8 / 8 times and each section index exactly 8 / 4 times. The requests that leave the groups of one section index for groups of one rep index name each section index exactly 8 / 4 times; the requests that leave the groups of one rep index for groups of one section index name each rep index exactly 8 / 8 times.
All inputs are finite; a program needn't handle non-finite values.
Results may differ from the reference program's by a relative error of at most 0.0049.
Values may be sent and summed in bfloat16 or wider, within the bound.
A program may use at most 64 MiB of HBM per device.

```python
import math
import jax
import jax.numpy as jnp
import numpy as np
from jax import lax

D = 6144
GATED_CHANNELS = 32
HD = 128
QHEADS = 64
KVHEADS = 8
REQ_DEV = 8
INPUT_SPAN = 256
STEPS = 4
GROUPS = 32
CLIENT_TOTAL = 256
TOTAL_TOKENS = 40960
N_REP = 8


def shared_keys(key):
    array_shape = (STEPS, CLIENT_TOTAL, KVHEADS * HD)
    normal_part = jnp.clip(jax.random.normal(key, array_shape, jnp.float32), -4.0, 4.0)
    return normal_part


def draw_soft_new_key(key, part):
    normal_part = shared_keys(key)
    return normal_part.astype(jnp.bfloat16)


def draw_soft_query(key, part):
    key = jax.random.fold_in(key, 4)
    own_part = jnp.clip(jax.random.normal(key, (STEPS, CLIENT_TOTAL, QHEADS, HD), jnp.float32), -4.0, 4.0)
    return own_part.reshape(STEPS, CLIENT_TOTAL, QHEADS * HD).astype(jnp.bfloat16)


def draw_decode_group(key, part):
    key = jax.random.fold_in(key, 5)
    seed_splits = jax.random.split(key, 3)
    section_count = GROUPS // N_REP
    section_order = jax.random.permutation(seed_splits[0], section_count)
    rep_order = jax.random.permutation(seed_splits[1], N_REP)
    scores = jax.random.randint(seed_splits[2], (GROUPS, REQ_DEV), 0, 1 << 20) * REQ_DEV + jnp.arange(REQ_DEV)[None, :]
    turns = jnp.argsort(scores, axis=1)
    group_ids = jnp.arange(GROUPS)[:, None]
    section_of = section_order[(group_ids // N_REP + turns) % section_count]
    rep_of = rep_order[(group_ids % N_REP + turns) % N_REP]
    return (section_of * N_REP + rep_of).reshape(CLIENT_TOTAL).astype(jnp.int32)


def draw_prefill_gate(key, part):
    key = jax.random.fold_in(key, 6)
    seed_splits = jax.random.split(key, 7)
    fast_share = 0.4
    is_fast = jax.random.uniform(seed_splits[0], (GATED_CHANNELS,)) < fast_share
    spans = jax.random.uniform(seed_splits[1], (GATED_CHANNELS,), jnp.float32, 30.0, 50.0)
    slow_rate = jax.random.uniform(seed_splits[2], (GATED_CHANNELS,), jnp.float32, 0.05, 0.5) / INPUT_SPAN
    forget_speeds = jnp.where(is_fast, 1.0 / spans, slow_rate)
    multiplier_coefficient = jnp.exp(jax.random.uniform(seed_splits[3], (CLIENT_TOTAL, 1, 1), jnp.float32, math.log(0.5), 0.0))
    spurt_widths = jax.random.uniform(seed_splits[4], (CLIENT_TOTAL, INPUT_SPAN, GATED_CHANNELS)) < 1.5 / INPUT_SPAN
    shrink_margin = jax.random.uniform(seed_splits[5], (CLIENT_TOTAL, INPUT_SPAN, GATED_CHANNELS), jnp.float32, 0.5, 0.8)
    gaussian_jitter = jax.random.uniform(seed_splits[6], (CLIENT_TOTAL, INPUT_SPAN, GATED_CHANNELS), jnp.float32, 0.7, 1.3)
    return jnp.exp(-forget_speeds[None, None, :] * multiplier_coefficient * gaussian_jitter) * jnp.where(spurt_widths, shrink_margin, 1.0)


def shard_levels(own_key, extent, shards, least, top_value):
    def one(dim, shards_of):
        steps = jax.random.uniform(jax.random.fold_in(jax.random.fold_in(own_key, 6), dim), (shards_of,), jnp.float32, least / len(shards), top_value / len(shards))
        return jnp.repeat(jnp.exp(steps), extent[dim] // shards_of).reshape((-1,) + (1,) * (len(extent) - dim - 1))

    loudness = one(*shards[0])
    for cut in shards[1:]:
        loudness = loudness * one(*cut)
    return loudness


def profile(amount, total, most, slope):
    weights = [(1 << 20) // math.isqrt(grade ** slope) + 1 for grade in range(2, amount + 1)]
    rest, counts = total - most - (amount - 1), [1] * (amount - 1)
    while rest > 0:
        candidates = [i for i in range(amount - 1) if counts[i] < most]
        mass, left = sum([weights[i] for i in candidates]), rest
        for i in candidates:
            more = min(most - counts[i], max(1, left * weights[i] // mass), rest)
            counts[i] = counts[i] + more
            rest = rest - more
    return np.array([most] + counts)


def uneven(own_key, number_of, total, limit, lean):
    if number_of == 2:
        one = jax.random.randint(own_key, (), max(1, total - limit), min(limit, total - 1) + 1)
        return jnp.stack([one, total - one])
    tallies = jnp.asarray(profile(number_of, total, limit, lean), jnp.int32)
    twos = (number_of - 1) // 2
    donor, receiver = tallies[1:1 + 2 * twos:2], tallies[2:2 + 2 * twos:2]
    room = jnp.minimum(donor - 1, limit - receiver)
    moved = jax.random.randint(jax.random.fold_in(own_key, 1), (twos,), 0, 1 << 20) % (room + 1)
    tallies = tallies.at[1:1 + 2 * twos:2].set(donor - moved).at[2:2 + 2 * twos:2].set(receiver + moved)
    return tallies[jax.random.permutation(jax.random.fold_in(own_key, 2), number_of)]


def gaussian(key, extent, deviation, reach, shards=(), kind=jnp.bfloat16):
    drawn = jax.random.normal(key, extent, jnp.float32) * deviation
    if len(shards) > 0:
        drawn = shard_levels(key, extent, shards, -0.22, 0.18) * drawn
    return jnp.clip(drawn, min=-reach, max=reach).astype(kind)


def setup_inputs(seed: int = 0) -> dict:
    arg_keys = jax.random.split(jax.random.key(seed), 19)
    return {
        "prefill_query": gaussian(arg_keys[0], (CLIENT_TOTAL, INPUT_SPAN, GATED_CHANNELS * HD), (2.0 / HD ** 0.5), 1.0546875, ((0, 32), (2, 8))),
        "prefill_key": gaussian(arg_keys[1], (CLIENT_TOTAL, INPUT_SPAN, GATED_CHANNELS * HD), (2.0 / HD ** 0.5), 1.0546875, ((0, 32), (2, 8))),
        "prefill_value": gaussian(arg_keys[2], (CLIENT_TOTAL, INPUT_SPAN, GATED_CHANNELS * HD), 1.0, 6.0, ((0, 32), (2, 8))),
        "prefill_gate": draw_prefill_gate(jax.random.fold_in(arg_keys[18], 71), 0),
        "lengths": uneven(arg_keys[4], CLIENT_TOTAL, TOTAL_TOKENS, INPUT_SPAN, 2).astype(jnp.int32),
        "decode_group": draw_decode_group(jax.random.fold_in(arg_keys[18], 71), 0),
        "cache_keys": gaussian(arg_keys[6], (CLIENT_TOTAL, INPUT_SPAN, KVHEADS * HD), 1.0, 6.0, ((0, 32), (2, 8))),
        "cache_values": gaussian(arg_keys[7], (CLIENT_TOTAL, INPUT_SPAN, KVHEADS * HD), 1.0, 6.0, ((0, 32), (2, 8))),
        "out_weight": gaussian(arg_keys[8], (GATED_CHANNELS * HD, D), (GATED_CHANNELS * HD) ** -0.5, 0.09375, ((0, 8),)),
        "norm_gain": jnp.clip(1.0 + 0.15 * jax.random.normal(arg_keys[9], (D,), jnp.float32), 0.25, 1.75),
        "step_input": gaussian(arg_keys[10], (STEPS, CLIENT_TOTAL, D), 0.5, 3.0, ((1, 32),)),
        "step_query": gaussian(arg_keys[11], (STEPS, CLIENT_TOTAL, GATED_CHANNELS * HD), (2.0 / HD ** 0.5), 1.0546875, ((1, 32), (2, 8))),
        "step_key": gaussian(arg_keys[12], (STEPS, CLIENT_TOTAL, GATED_CHANNELS * HD), (2.0 / HD ** 0.5), 1.0546875, ((1, 32), (2, 8))),
        "step_value": gaussian(arg_keys[13], (STEPS, CLIENT_TOTAL, GATED_CHANNELS * HD), 1.0, 6.0, ((1, 32), (2, 8))),
        "step_gate": jnp.clip(0.5 + 0.5 * jax.random.uniform(arg_keys[14], (STEPS, CLIENT_TOTAL, GATED_CHANNELS), jnp.float32) ** shard_levels(arg_keys[14], (STEPS, CLIENT_TOTAL, GATED_CHANNELS), ((1, 32), (2, 8)), -0.2, 0.2), 0.5, 1.0),
        "soft_query": draw_soft_query(jax.random.fold_in(arg_keys[18], 71), 0),
        "soft_new_key": draw_soft_new_key(jax.random.fold_in(arg_keys[18], 71), 0),
        "soft_new_value": gaussian(arg_keys[17], (STEPS, CLIENT_TOTAL, KVHEADS * HD), 1.0, 6.0, ((1, 32), (2, 8))),
    }


HIGHEST = lax.Precision.HIGHEST

def decode_slots(decode_group):
    numbers = jnp.arange(CLIENT_TOTAL, dtype=jnp.int32)
    same_group = decode_group[None, :] == decode_group[:, None]
    earlier = numbers[None, :] < numbers[:, None]
    ranking = lax.optimization_barrier(jnp.sum((same_group & earlier).astype(jnp.int32), axis=1)).astype(jnp.int32)
    slot_of = (decode_group * REQ_DEV + ranking).astype(jnp.int32)
    landing = slot_of[None, :] == numbers[:, None]
    return lax.optimization_barrier(jnp.sum(jnp.where(landing, numbers[None, :], 0), axis=1)).astype(jnp.int32)

def log_decay(gates, length):
    places = jnp.arange(INPUT_SPAN, dtype=jnp.int32)
    inside = places < length
    logs = jnp.where(inside[:, None], jnp.log(gates), 0.0)
    return (inside, jnp.cumsum(logs, axis=0))

def prefill_output(query_rows, key_rows, value_rows, gates, length):
    queries = query_rows.reshape(INPUT_SPAN, GATED_CHANNELS, HD).astype(jnp.float32)
    keys_all = key_rows.reshape(INPUT_SPAN, GATED_CHANNELS, HD).astype(jnp.float32)
    values_all = value_rows.reshape(INPUT_SPAN, GATED_CHANNELS, HD).astype(jnp.float32)
    inside, cumlog = log_decay(gates, length)
    scores = jnp.einsum('thd,shd->hts', queries, keys_all, precision=HIGHEST)
    heads_first = cumlog.T
    gaps = heads_first[:, :, None] - heads_first[:, None, :]
    places = jnp.arange(INPUT_SPAN, dtype=jnp.int32)
    causal = places[:, None] >= places[None, :]
    keeping = causal[None] & inside[None, None, :] & inside[None, :, None]
    weights = jnp.where(keeping, jnp.exp(jnp.where(keeping, gaps, 0.0)) * scores, 0.0).astype(jnp.bfloat16)
    weights = lax.optimization_barrier(weights)
    outputs = jnp.einsum('hts,shd->thd', weights.astype(jnp.float32), values_all, precision=HIGHEST)
    return outputs.reshape(INPUT_SPAN, GATED_CHANNELS * HD).astype(jnp.bfloat16)

def prefill_memory(key_rows, value_rows, gates, length):
    keys_all = key_rows.reshape(INPUT_SPAN, GATED_CHANNELS, HD).astype(jnp.float32)
    values_all = value_rows.reshape(INPUT_SPAN, GATED_CHANNELS, HD).astype(jnp.float32)
    inside, cumlog = log_decay(gates, length)
    decays = jnp.where(inside[:, None], jnp.exp(cumlog[-1][None, :] - cumlog), 0.0)
    return jnp.einsum('sh,shd,she->hde', decays, keys_all, values_all, precision=HIGHEST)

def reference(prefill_query, prefill_key, prefill_value, prefill_gate, lengths, decode_group, cache_keys, cache_values, out_weight, norm_gain, step_input, step_query, step_key, step_value, step_gate, soft_query, soft_new_key, soft_new_value):

    def prompt_one(request):
        return prefill_output(prefill_query[request], prefill_key[request], prefill_value[request], prefill_gate[request], lengths[request])
    prefill_out = lax.map(prompt_one, jnp.arange(CLIENT_TOTAL, dtype=jnp.int32))
    request_of = decode_slots(decode_group)
    score_scale = 1.0 / math.sqrt(HD)

    def one_slot(slot_no):
        request = request_of[slot_no]
        length = lengths[request]
        carried = prefill_memory(prefill_key[request], prefill_value[request], prefill_gate[request], length)
        cache_k = cache_keys[request].reshape(INPUT_SPAN, KVHEADS, HD).astype(jnp.float32)
        cache_v = cache_values[request].reshape(INPUT_SPAN, KVHEADS, HD).astype(jnp.float32)
        fresh_k = soft_new_key[:, slot_no].reshape(STEPS, KVHEADS, HD).astype(jnp.float32)
        fresh_v = soft_new_value[:, slot_no].reshape(STEPS, KVHEADS, HD).astype(jnp.float32)
        cache_ok = jnp.arange(INPUT_SPAN, dtype=jnp.int32) < length
        linear_rows = []
        soft_rows = []
        for step_no in range(STEPS):
            gates_now = step_gate[step_no, slot_no]
            key_now = step_key[step_no, slot_no].reshape(GATED_CHANNELS, HD).astype(jnp.float32)
            value_now = step_value[step_no, slot_no].reshape(GATED_CHANNELS, HD).astype(jnp.float32)
            query_now = step_query[step_no, slot_no].reshape(GATED_CHANNELS, HD).astype(jnp.float32)
            carried = gates_now[:, None, None] * carried + key_now[:, :, None] * value_now[:, None, :]
            linear = jnp.einsum('hd,hde->he', query_now, carried, precision=HIGHEST)
            linear_rows.append(linear.reshape(GATED_CHANNELS * HD).astype(jnp.bfloat16))
            asked = soft_query[step_no, slot_no].reshape(KVHEADS, QHEADS // KVHEADS, HD).astype(jnp.float32)
            cache_scores = jnp.einsum('kgd,skd->kgs', asked, cache_k, precision=HIGHEST) * score_scale
            fresh_scores = jnp.einsum('kgd,nkd->kgn', asked, fresh_k, precision=HIGHEST) * score_scale
            cache_scores = jnp.where(cache_ok, cache_scores, -jnp.inf)
            fresh_ok = jnp.arange(STEPS, dtype=jnp.int32) <= step_no
            fresh_scores = jnp.where(fresh_ok, fresh_scores, -jnp.inf)
            peaks = jnp.maximum(lax.optimization_barrier(jnp.max(cache_scores, axis=-1)), lax.optimization_barrier(jnp.max(fresh_scores, axis=-1)))
            cache_exp = jnp.exp(cache_scores - peaks[..., None])
            fresh_exp = jnp.exp(fresh_scores - peaks[..., None])
            denominator = lax.optimization_barrier(jnp.sum(cache_exp, axis=-1)) + lax.optimization_barrier(jnp.sum(fresh_exp, axis=-1))
            cache_prob = (cache_exp / denominator[..., None]).astype(jnp.bfloat16)
            fresh_prob = (fresh_exp / denominator[..., None]).astype(jnp.bfloat16)
            cache_prob, fresh_prob = lax.optimization_barrier((cache_prob, fresh_prob))
            mixed = jnp.einsum('kgs,skd->kgd', cache_prob.astype(jnp.float32), cache_v, precision=HIGHEST)
            mixed = mixed + jnp.einsum('kgn,nkd->kgd', fresh_prob.astype(jnp.float32), fresh_v, precision=HIGHEST)
            soft_rows.append(mixed.reshape(QHEADS * HD).astype(jnp.bfloat16))
        return (jnp.stack(linear_rows), jnp.stack(soft_rows))
    linear_all, soft_all = lax.map(one_slot, jnp.arange(CLIENT_TOTAL, dtype=jnp.int32))
    linear_all = jnp.swapaxes(linear_all, 0, 1)
    soft_out = jnp.swapaxes(soft_all, 0, 1)
    projected = jnp.dot(linear_all.reshape(STEPS * CLIENT_TOTAL, GATED_CHANNELS * HD), out_weight, preferred_element_type=jnp.float32)
    summed = step_input.reshape(STEPS * CLIENT_TOTAL, D).astype(jnp.float32) + projected
    spread = jnp.sqrt(lax.optimization_barrier(jnp.mean(summed * summed, axis=-1, keepdims=True)) + 1e-06)
    decode_out = (summed / spread * norm_gain).astype(jnp.bfloat16).reshape(STEPS, CLIENT_TOTAL, D)
    return (prefill_out, decode_out, soft_out)
```

```python
import functools
import math

import jax
import jax.numpy as jnp
from jax import lax
from jax.experimental import pallas as pl
from jax.experimental.pallas import tpu as pltpu
from jax.sharding import PartitionSpec as P

MESH = pl.DeviceIdType.MESH
F32 = jnp.float32
BF16 = jnp.bfloat16
LOG2E = 1.0 / math.log(2.0)
LANES = 128


def iota(shape, axis):
    return lax.broadcasted_iota(jnp.int32, shape, axis)


def dot(a, b):
    return jnp.dot(a, b, preferred_element_type=F32)


def dot_nt(a, b, precision=None):
    return lax.dot_general(
        a, b, (((1,), (1,)), ((), ())), preferred_element_type=F32, precision=precision
    )


def one_hot(mask):
    return jnp.where(mask, 1.0, 0.0).astype(BF16)


def split_two(x):
    high = x.astype(BF16)
    return high, (x - high.astype(F32)).astype(BF16)


def body(
    dims,
    pq_hbm,
    pk_hbm,
    pv_hbm,
    gate_hbm,
    len_hbm,
    dg_hbm,
    dgv_hbm,
    ck_hbm,
    cv_hbm,
    w_hbm,
    gain_hbm,
    si_hbm,
    sq_hbm,
    sk_hbm,
    sv_hbm,
    sg_hbm,
    fq_hbm,
    fk_hbm,
    fv_hbm,
    po_hbm,
    do_hbm,
    so_hbm,
    pq,
    pk,
    pv,
    gate,
    len_s,
    dg_s,
    dgv,
    ck,
    cv,
    w,
    gain,
    si,
    sq,
    sk,
    sv,
    sg,
    fq,
    fk,
    fv,
    po,
    so,
    rowf,
    decf,
    colm,
    own,
    gamma,
    sel_lin,
    sel_soft,
    send_q,
    recv_q,
    res_q,
    send_r,
    recv_r,
    send_s,
    recv_s,
    res_s,
    send_t,
    recv_t,
    part_f,
    part_b,
    recv_p,
    ss_send,
    ss_recv,
    ag,
    in_sem,
    out_sem,
    q_sem,
    r_sem,
    s_sem,
    t_sem,
    rs_send,
    rs_recv,
    sib_sem,
    ag_send,
    ag_recv,
):
    sections, reps, tps, held, length, heads, steps, q_heads, model = dims
    groups = sections * reps
    total = groups * held
    me_s = lax.axis_index("section")
    me_r = lax.axis_index("rep")
    me_p = lax.axis_index("tp")
    me_g = me_s * reps + me_r
    first = me_g * held
    half = model // 2
    per_owner = steps * 2 // tps
    me_y = me_p // 2
    me_c = me_p % 2
    lin_rows = heads * steps
    soft_rows = q_heads * steps

    barrier = pltpu.get_barrier_semaphore()

    def greet(off, carry):
        peer = lax.rem(me_g + off, groups)
        pl.semaphore_signal(
            barrier, inc=1, device_id=(peer // reps, lax.rem(peer, reps), me_p), device_id_type=MESH
        )
        return carry

    lax.fori_loop(1, groups, greet, 0)

    def greet_tp(off, carry):
        pl.semaphore_signal(
            barrier,
            inc=1,
            device_id=(me_s, me_r, lax.rem(me_p + off, tps)),
            device_id_type=MESH,
        )
        return carry

    lax.fori_loop(1, tps, greet_tp, 0)

    y0 = me_y * per_owner
    col0 = pl.multiple_of(me_c * half, LANES)
    loads = {}
    for place, (name, src, dst) in enumerate(
        (
            ("dgv", dgv_hbm, dgv),
            ("sq", sq_hbm, sq),
            ("dg", dg_hbm, dg_s),
            ("len", len_hbm, len_s),
            ("gate", gate_hbm, gate),
            ("pk", pk_hbm, pk),
            ("pv", pv_hbm, pv),
            ("pq", pq_hbm, pq),
            ("fq", fq_hbm, fq),
            ("fk", fk_hbm, fk),
            ("fv", fv_hbm, fv),
            ("sk", sk_hbm, sk),
            ("sv", sv_hbm, sv),
            ("sg", sg_hbm, sg),
            ("w", w_hbm, w),
            ("ck", ck_hbm, ck),
            ("cv", cv_hbm, cv),
            ("si", si_hbm.at[pl.ds(y0, per_owner), :, pl.ds(col0, half)], si),
            ("gain", gain_hbm.at[:, pl.ds(col0, half)], gain),
        )
    ):
        loads[name] = pltpu.make_async_copy(src, dst, in_sem.at[place])
        loads[name].start()

    loads["dgv"].wait()
    mine = dgv[...] == me_g
    mine_rows = jnp.broadcast_to(one_hot(mine), (16, total))
    before = one_hot(iota((total, total), 0) < iota((total, total), 1))
    rank = dot(mine_rows, before)[0:1]
    slot_row = lax.rem(iota((soft_rows * held, total), 0), held).astype(F32)
    slot_of = one_hot(jnp.where(mine, rank, -1.0) == slot_row)
    slot_lin = slot_of[: lin_rows * held]

    def rep_rows(rows_each):
        shape = (rows_each * reps, total)
        source_rep = lax.rem(iota(shape, 1) // held, reps)
        return one_hot(iota(shape, 0) // rows_each == source_rep)

    def spread(rows_each, slots):
        picked = dot_nt(rep_rows(rows_each), slots)
        same = lax.rem(iota(picked.shape, 0), rows_each) == iota(picked.shape, 1) // held
        return jnp.where(same, picked, 0.0).astype(BF16)

    def by_row(ref, count):
        pieces = [
            ref[i, :, a * LANES : (a + 1) * LANES].astype(F32)
            for a in range(count)
            for i in range(steps)
        ]
        return jnp.concatenate(pieces, axis=0).astype(BF16)

    loads["sq"].wait()
    spread_lin = spread(lin_rows, slot_lin)
    blocks = dot(spread_lin, by_row(sq, heads)).astype(BF16)
    send_q[...] = blocks.reshape(reps, lin_rows, LANES)

    pl.semaphore_wait(barrier, groups - 1 + tps - 1)

    def to_groups(src, dst, sems):
        def one(off, carry):
            peer = lax.rem(me_g + off, groups)
            peer_r = lax.rem(peer, reps)
            pltpu.make_async_remote_copy(
                src_ref=src.at[peer_r],
                dst_ref=dst.at[me_g],
                send_sem=sems.at[0],
                recv_sem=sems.at[1],
                device_id=(peer // reps, peer_r, me_p),
                device_id_type=MESH,
            ).start()
            return carry

        lax.fori_loop(1, groups, one, 0)
        dst[me_g] = src[me_r]

    def all_bytes(dst, sem):
        view = dst.at[pl.ds(0, groups - 1)]
        pltpu.make_async_copy(view, view, sem).wait()

    to_groups(send_q, recv_q, q_sem)

    loads["dg"].wait()
    loads["len"].wait()
    loads["gate"].wait()
    count = held * heads
    shape = (count, length)
    own_len = [len_s[first + k] for k in range(held)]
    logs = jnp.log(jnp.concatenate([gate[k] for k in range(held)], axis=0))
    len_rows = jnp.zeros(shape, jnp.int32)
    for k in range(held):
        len_rows = jnp.where(iota(shape, 0) // heads == k, own_len[k], len_rows)
    inside = iota(shape, 1) < len_rows
    logs = jnp.where(inside, logs, 0.0)
    p1, rest = split_two(logs)
    rest = logs - p1.astype(F32)
    p2, p3 = split_two(rest)
    upto = one_hot(iota((length, length), 0) <= iota((length, length), 1))
    upto_t = one_hot(iota((length, length), 1) <= iota((length, length), 0))
    cum_rows = (dot(p1, upto) + dot(p2, upto) + dot(p3, upto)) * LOG2E
    cum_cols = (dot_nt(upto_t, p1) + dot_nt(upto_t, p2) + dot_nt(upto_t, p3)) * LOG2E
    decays = jnp.where(inside, jnp.exp2(cum_rows[:, length - 1 :] - cum_rows), 0.0)
    shape = (length, count)
    len_cols = jnp.zeros(shape, jnp.int32)
    for k in range(held):
        len_cols = jnp.where(iota(shape, 1) // heads == k, own_len[k], len_cols)
    cum_cols = jnp.where(iota(shape, 0) < len_cols, cum_cols, -jnp.inf)
    for k in range(held):
        rows = slice(k * heads, (k + 1) * heads)
        rowf[k] = cum_rows[rows]
        decf[k] = decays[rows]
        colm[k] = cum_cols[:, rows]

    loads["pk"].wait()
    loads["pv"].wait()
    loads["pq"].wait()
    mid = length // 2

    def prompt(k, carry):
        causal = iota((mid, mid), 0) >= iota((mid, mid), 1)
        for h in range(heads):
            lanes = slice(h * LANES, (h + 1) * LANES)
            scores = dot_nt(pq[k, :, lanes], pk[k, :, lanes])
            row = rowf[k, h : h + 1, :]
            col = colm[k, :, h : h + 1]
            values = pv[k, :, lanes]
            gap = jnp.where(causal, col[:mid] - row[:, :mid], -jnp.inf)
            top = (jnp.exp2(gap) * scores[:mid, :mid]).astype(BF16)
            low_left = (jnp.exp2(col[mid:] - row[:, :mid]) * scores[mid:, :mid]).astype(BF16)
            gap = jnp.where(causal, col[mid:] - row[:, mid:], -jnp.inf)
            low_right = (jnp.exp2(gap) * scores[mid:, mid:]).astype(BF16)
            low = jnp.concatenate([low_left, low_right], axis=1)
            po[k, :mid, lanes] = dot(top, values[:mid]).astype(BF16)
            po[k, mid:, lanes] = dot(low, values).astype(BF16)
        pltpu.make_async_copy(po.at[k], po_hbm.at[k], out_sem.at[k]).start()
        return carry

    marks = [0, held // 4, held // 2 + 1, held // 2 + 2, held]
    lax.fori_loop(marks[0], marks[1], prompt, 0)

    for name in ("fq", "fk", "fv", "sk", "sv", "sg"):
        loads[name].wait()
    soft_blocks = dot(spread(soft_rows, slot_of), by_row(fq, q_heads)).astype(BF16)
    send_s[:, :soft_rows, :] = soft_blocks.reshape(reps, soft_rows, LANES)
    fresh = jnp.concatenate([by_row(fk, 1).astype(F32), by_row(fv, 1).astype(F32)], axis=0)
    fresh_spread = spread_lin[:, : 2 * steps * held]
    fresh_blocks = dot(fresh_spread, fresh.astype(BF16)).astype(BF16)
    send_s[:, soft_rows:, :] = fresh_blocks.reshape(reps, lin_rows, LANES)

    target_rep = [lax.rem(dg_s[first + k], reps) for k in range(held)]
    bound_for = []
    for r in range(reps):
        found = jnp.int32(0)
        for k in range(held):
            found = jnp.where(target_rep[k] == r, k, found)
        bound_for.append(found)
    all_bytes(recv_q, q_sem.at[1])
    head_of_row = iota((lin_rows, length), 0) // steps
    for k in range(held):
        asked = recv_q[dg_s[first + k]]
        result = jnp.zeros((2 * lin_rows, LANES), F32)
        for h in range(heads):
            lanes = slice(h * LANES, (h + 1) * LANES)
            weights = dot_nt(asked, pk[k, :, lanes]) * decf[k, h : h + 1, :]
            high, low = split_two(jnp.where(head_of_row == h, weights, 0.0))
            result = result + dot(jnp.concatenate([high, low], axis=0), pv[k, :, lanes])
        res_q[k] = (result[:lin_rows] + result[lin_rows:]).astype(BF16)
    for r in range(reps):
        send_r[r] = res_q[bound_for[r]]
    to_groups(send_r, recv_r, r_sem)
    to_groups(send_s, recv_s, s_sem)

    eye = jnp.where(iota((held, held), 0) == iota((held, held), 1), 1.0, 0.0)
    gates = [dot_nt(eye, sg[i], lax.Precision.HIGHEST) for i in range(steps)]
    for h in range(heads):
        lanes = slice(h * LANES, (h + 1) * LANES)
        running = jnp.ones((held, 1), F32)
        for i in range(steps):
            running = running * gates[i][:, h : h + 1]
            gamma[i, :, lanes] = jnp.broadcast_to(running, (held, LANES))
            query = sq[i, :, lanes].astype(F32)
            added = jnp.zeros((held, LANES), F32)
            since = jnp.ones((held, 1), F32)
            for u in range(i, -1, -1):
                pair = jnp.sum(query * sk[u, :, lanes].astype(F32), axis=1, keepdims=True)
                added = added + (since * pair) * sv[u, :, lanes].astype(F32)
                since = since * gates[u][:, h : h + 1]
            own[i, :, lanes] = added

    def pick(rows_each, slots):
        shape = (total, rows_each * groups)
        source = one_hot(iota(shape, 0) // held == iota(shape, 1) // rows_each)
        picked = dot(slots, source)
        same = iota(picked.shape, 0) // held == lax.rem(iota(picked.shape, 1), rows_each)
        return jnp.where(same, picked, 0.0).astype(BF16)

    sel_lin[...] = pick(lin_rows, slot_lin)
    lax.fori_loop(marks[1], marks[2], prompt, 0)

    loads["w"].wait()
    all_bytes(recv_r, r_sem.at[1])
    carried = dot(sel_lin[...], recv_r[...].reshape(groups * lin_rows, LANES))
    hidden = []
    for i in range(steps):
        across = []
        for h in range(heads):
            lanes = slice(h * LANES, (h + 1) * LANES)
            rows = slice((h * steps + i) * held, (h * steps + i + 1) * held)
            across.append(gamma[i, :, lanes] * carried[rows] + own[i, :, lanes])
        hidden.append(jnp.concatenate(across, axis=1))
    hidden = jnp.concatenate(hidden, axis=0).astype(BF16)
    pieces = 4
    wide = model // pieces
    owners = tps // 2

    def piece_copy(c, owner, source):
        return pltpu.make_async_remote_copy(
            src_ref=part_b.at[pl.ds(owner * per_owner, per_owner), :, c * wide : (c + 1) * wide],
            dst_ref=recv_p.at[source, c % 2],
            send_sem=rs_send.at[owner, c],
            recv_sem=rs_recv.at[source, c % 2],
            device_id=(me_s, me_r, owner * 2 + c // 2),
            device_id_type=MESH,
        )

    for c in range(pieces):
        cols = slice(c * wide, (c + 1) * wide)
        partial = dot(hidden, w[:, cols])
        for i in range(steps):
            rows = partial[i * held : (i + 1) * held]
            part_f[i, :, cols] = rows
            part_b[i, :, cols] = rows.astype(BF16)

        for off in range(owners):
            owner = lax.rem(me_y + 1 + off, owners)

            @pl.when((owner != me_y) | (me_c != c // 2))
            def _():
                piece_copy(c, owner, me_p).start()

    loads["ck"].wait()
    loads["cv"].wait()
    all_bytes(recv_s, s_sem.at[1])
    scale = LOG2E / math.sqrt(LANES)

    def soft(k, carry):
        block = recv_s[dg_s[first + k]]
        asked = block[:soft_rows]
        fresh_rows = block[soft_rows:]
        scores = dot_nt(asked, ck[k]) * scale
        scores = jnp.where(iota(scores.shape, 1) < len_s[first + k], scores, -jnp.inf)
        news = dot_nt(asked, fresh_rows) * scale
        lane = iota(news.shape, 1)
        seen = (lane < steps) & (lane <= lax.rem(iota(news.shape, 0), steps))
        news = jnp.where(seen, news, -jnp.inf)
        peak = jnp.maximum(
            jnp.max(scores, axis=1, keepdims=True), jnp.max(news, axis=1, keepdims=True)
        )
        scores = jnp.exp2(scores - peak)
        news = jnp.exp2(news - peak)
        bottom = jnp.sum(scores, axis=1, keepdims=True) + jnp.sum(news, axis=1, keepdims=True)
        probs = (scores / bottom).astype(BF16)
        fresh_probs = (news / bottom).astype(BF16).astype(F32)
        fresh_values = fresh_rows.astype(F32)
        mixed = dot(probs, cv[k])
        for u in range(steps):
            mixed = mixed + fresh_probs[:, u : u + 1] * fresh_values[steps + u : steps + u + 1]
        res_s[k] = mixed.astype(BF16)
        return carry

    lax.fori_loop(0, held, soft, 0)
    for r in range(reps):
        send_t[r] = res_s[bound_for[r]]
    to_groups(send_t, recv_t, t_sem)
    sel_soft[...] = pick(soft_rows, slot_of)

    loads["si"].wait()
    loads["gain"].wait()
    summed = []
    for part in range(2):
        cols = pl.ds(pl.multiple_of(me_c * half + part * wide, LANES), wide)
        here = slice(part * wide, (part + 1) * wide)
        value = part_f[pl.ds(y0, per_owner), :, cols] + si[:, :, here].astype(F32)
        for off in range(1, tps):
            source = lax.rem(me_p + off, tps)
            pltpu.make_async_copy(
                recv_p.at[source, part], recv_p.at[source, part], rs_recv.at[source, part]
            ).wait()
            value = value + recv_p[source, part].astype(F32)
        summed.append(value)
    square = jnp.sum(summed[0] * summed[0], axis=2, keepdims=True)
    square = square + jnp.sum(summed[1] * summed[1], axis=2, keepdims=True)
    ss_send[...] = jnp.broadcast_to(square, ss_send.shape)
    sibling = pltpu.make_async_remote_copy(
        src_ref=ss_send,
        dst_ref=ss_recv,
        send_sem=sib_sem.at[0],
        recv_sem=sib_sem.at[1],
        device_id=(me_s, me_r, me_p + 1 - 2 * me_c),
        device_id_type=MESH,
    )
    sibling.start()
    sibling.wait()
    mean = (square + ss_recv[:, :, 0:1]) / model
    spread_of = jnp.sqrt(mean + 1e-06)
    for part in range(2):
        here = slice(part * wide, (part + 1) * wide)
        gains = gain[:, here].reshape(1, 1, wide)
        ag[:, :, here] = (summed[part] / spread_of * gains).astype(BF16)
    place = do_hbm.at[pl.ds(y0, per_owner), :, pl.ds(col0, half)]
    mine_out = pltpu.make_async_copy(ag, place, out_sem.at[held])
    mine_out.start()

    def gather_copy(peer):
        return pltpu.make_async_remote_copy(
            src_ref=ag,
            dst_ref=place,
            send_sem=ag_send.at[peer],
            recv_sem=ag_recv.at[me_p],
            device_id=(me_s, me_r, peer),
            device_id_type=MESH,
        )

    for off in range(1, tps):
        gather_copy(lax.rem(me_p + off, tps)).start()

    lax.fori_loop(marks[2], marks[4], prompt, 0)

    all_bytes(recv_t, t_sem.at[1])
    placed = dot(sel_soft[...], recv_t[...].reshape(groups * soft_rows, LANES))
    for a in range(q_heads):
        for i in range(steps):
            rows = slice((a * steps + i) * held, (a * steps + i + 1) * held)
            so[i, :, a * LANES : (a + 1) * LANES] = placed[rows].astype(BF16)
    soft_out = pltpu.make_async_copy(so, so_hbm, out_sem.at[held + 1])
    soft_out.start()

    all_bytes(recv_q, q_sem.at[0])
    all_bytes(recv_r, r_sem.at[0])
    all_bytes(recv_s, s_sem.at[0])
    all_bytes(recv_t, t_sem.at[0])
    for c in range(pieces):
        for off in range(owners):
            owner = lax.rem(me_y + 1 + off, owners)

            @pl.when((owner != me_y) | (me_c != c // 2))
            def _():
                piece_copy(c, owner, me_p).wait_send()

    for k in range(held):
        pltpu.make_async_copy(po.at[k], po_hbm.at[k], out_sem.at[k]).wait()
    soft_out.wait()
    mine_out.wait()
    for off in range(1, tps):
        peer = lax.rem(me_p + off, tps)
        gather_copy(peer).wait_send()
        pltpu.make_async_copy(ag, ag, ag_recv.at[peer]).wait()


def on_device(
    prefill_query,
    prefill_key,
    prefill_value,
    prefill_gate,
    lengths,
    decode_group,
    cache_keys,
    cache_values,
    out_weight,
    norm_gain,
    step_input,
    step_query,
    step_key,
    step_value,
    step_gate,
    soft_query,
    soft_new_key,
    soft_new_value,
):
    sections, reps, tps = (lax.axis_size(name) for name in ("section", "rep", "tp"))
    held, length, heads = prefill_gate.shape
    steps = step_query.shape[0]
    q_heads = soft_query.shape[2] // LANES
    model = out_weight.shape[1]
    groups = sections * reps
    width = heads * LANES
    half = model // 2
    per_owner = steps * 2 // tps
    lin_rows = heads * steps
    soft_rows = q_heads * steps
    total = groups * held
    dims = (sections, reps, tps, held, length, heads, steps, q_heads, model)
    operands = (
        prefill_query,
        prefill_key,
        prefill_value,
        jnp.transpose(prefill_gate, (0, 2, 1)),
        lengths,
        decode_group,
        decode_group.reshape(1, total),
        cache_keys,
        cache_values,
        out_weight,
        norm_gain.reshape(1, model),
        step_input,
        step_query,
        step_key,
        step_value,
        jnp.transpose(step_gate, (0, 2, 1)),
        soft_query,
        soft_new_key,
        soft_new_value,
    )
    vmem = pltpu.VMEM
    dma = pltpu.SemaphoreType.DMA
    scratch = [
        vmem((held, length, width), BF16),
        vmem((held, length, width), BF16),
        vmem((held, length, width), BF16),
        vmem((held, heads, length), F32),
        pltpu.SMEM((total,), jnp.int32),
        pltpu.SMEM((total,), jnp.int32),
        vmem((1, total), jnp.int32),
        vmem((held, length, LANES), BF16),
        vmem((held, length, LANES), BF16),
        vmem((width, model), BF16),
        vmem((1, half), F32),
        vmem((per_owner, held, half), BF16),
        vmem((steps, held, width), BF16),
        vmem((steps, held, width), BF16),
        vmem((steps, held, width), BF16),
        vmem((steps, heads, held), F32),
        vmem((steps, held, q_heads * LANES), BF16),
        vmem((steps, held, LANES), BF16),
        vmem((steps, held, LANES), BF16),
        vmem((held, length, width), BF16),
        vmem((steps, held, q_heads * LANES), BF16),
        vmem((held, heads, length), F32),
        vmem((held, heads, length), F32),
        vmem((held, length, heads), F32),
        vmem((steps, held, width), F32),
        vmem((steps, held, width), F32),
        vmem((lin_rows * held, lin_rows * groups), BF16),
        vmem((soft_rows * held, soft_rows * groups), BF16),
        vmem((reps, lin_rows, LANES), BF16),
        vmem((groups, lin_rows, LANES), BF16),
        vmem((held, lin_rows, LANES), BF16),
        vmem((reps, lin_rows, LANES), BF16),
        vmem((groups, lin_rows, LANES), BF16),
        vmem((reps, soft_rows + lin_rows, LANES), BF16),
        vmem((groups, soft_rows + lin_rows, LANES), BF16),
        vmem((held, soft_rows, LANES), BF16),
        vmem((reps, soft_rows, LANES), BF16),
        vmem((groups, soft_rows, LANES), BF16),
        vmem((steps, held, model), F32),
        vmem((steps, held, model), BF16),
        vmem((tps, 2, per_owner, held, half // 2), BF16),
        vmem((per_owner, held, LANES), F32),
        vmem((per_owner, held, LANES), F32),
        vmem((per_owner, held, half), BF16),
        dma((19,)),
        dma((held + 2,)),
        dma((2,)),
        dma((2,)),
        dma((2,)),
        dma((2,)),
        dma((tps // 2, 4)),
        dma((tps, 2)),
        dma((2,)),
        dma((tps,)),
        dma((tps,)),
    ]
    anywhere = pl.BlockSpec(memory_space=pl.ANY)
    return pl.pallas_call(
        functools.partial(body, dims),
        out_shape=(
            jax.ShapeDtypeStruct((held, length, width), BF16),
            jax.ShapeDtypeStruct((steps, held, model), BF16),
            jax.ShapeDtypeStruct((steps, held, q_heads * LANES), BF16),
        ),
        in_specs=[anywhere] * len(operands),
        out_specs=(anywhere,) * 3,
        scratch_shapes=scratch,
        compiler_params=pltpu.CompilerParams(
            collective_id=0, has_side_effects=True, vmem_limit_bytes=56 * 1024 * 1024
        ),
    )(*operands)


def solution(mesh):
    rows = P(("section", "rep"), None, "tp")
    slots = P(None, ("section", "rep"), "tp")
    whole = P(None, ("section", "rep"), None)
    return jax.shard_map(
        on_device,
        mesh=mesh,
        in_specs=(
            rows,
            rows,
            rows,
            rows,
            P(),
            P(),
            rows,
            rows,
            P("tp", None),
            P(),
            whole,
            slots,
            slots,
            slots,
            slots,
            slots,
            slots,
            slots,
        ),
        out_specs=(rows, whole, slots),
        check_vma=False,
    )
```

```python
import functools
import math

import jax
import jax.numpy as jnp
from jax import lax
from jax.experimental import pallas as pl
from jax.experimental.pallas import tpu as pltpu
from jax.sharding import PartitionSpec as P

MESH = pl.DeviceIdType.MESH
F32 = jnp.float32
BF16 = jnp.bfloat16
LOG2E = 1.0 / math.log(2.0)
LANES = 128


def iota(shape, axis):
    return lax.broadcasted_iota(jnp.int32, shape, axis)


def dot(a, b):
    return jnp.dot(a, b, preferred_element_type=F32)


def dot_nt(a, b, precision=None):
    return lax.dot_general(
        a, b, (((1,), (1,)), ((), ())), preferred_element_type=F32, precision=precision
    )


def one_hot(mask):
    return jnp.where(mask, 1.0, 0.0).astype(BF16)


def split_two(x):
    high = x.astype(BF16)
    return high, (x - high.astype(F32)).astype(BF16)


def body(
    dims,
    pq_hbm,
    pk_hbm,
    pv_hbm,
    gate_hbm,
    len_hbm,
    dg_hbm,
    dgv_hbm,
    ck_hbm,
    cv_hbm,
    w_hbm,
    gain_hbm,
    si_hbm,
    sq_hbm,
    sk_hbm,
    sv_hbm,
    sg_hbm,
    fq_hbm,
    fk_hbm,
    fv_hbm,
    po,
    do,
    so,
    pq,
    pk,
    pv,
    gate,
    len_s,
    dg_s,
    dgv,
    ck,
    cv,
    w,
    gain,
    si,
    sq,
    sk,
    sv,
    sg,
    fq,
    fk,
    fv,
    rowf,
    colm,
    colw,
    state,
    own,
    gamma,
    sel_lin,
    sel_soft,
    send_q,
    recv_q,
    res_q,
    send_r,
    recv_r,
    send_s,
    recv_a,
    send_b,
    recv_b,
    res_s,
    send_t,
    recv_t,
    part_f,
    part_b,
    recv_p,
    ss_send,
    ss_recv,
    in_sem,
    q_sem,
    r_sem,
    a_sem,
    b_sem,
    t_sem,
    rs_send,
    rs_recv,
    ss_sem,
    ag_send,
    ag_recv,
    pass_send,
    pass_recv,
):
    sections, reps, tps, held, length, heads, steps, q_heads, model = dims
    groups = sections * reps
    total = groups * held
    me_s = lax.axis_index("section")
    me_r = lax.axis_index("rep")
    me_p = lax.axis_index("tp")
    me_g = me_s * reps + me_r
    first = me_g * held
    half = model // 2
    per_owner = steps * 2 // tps
    me_y = me_p // 2
    me_c = me_p % 2
    lin_rows = heads * steps
    soft_rows = q_heads * steps

    owners = tps // 2
    sibling = (me_s, me_r, me_p + 1 - 2 * me_c)

    deep = 2 * sections
    across = reps // 2
    me_z = (me_r // across) * sections + me_s
    me_x = lax.rem(me_r, across)

    def ring_step(n, size):
        return size // 2 + ((n + 1) // 2) * (1 - 2 * lax.rem(n, 2)) + size

    def far_first(m):
        z = lax.rem(me_z + ring_step(m // across, deep), deep)
        x = lax.rem(me_x + ring_step(lax.rem(m, across), across), across)
        return lax.rem(z, sections), (z // sections) * across + x

    def along_y(off):
        return lax.rem(me_y + off, owners)

    barrier = pltpu.get_barrier_semaphore()

    def greet(m, carry):
        peer_s, peer_r = far_first(m)
        pl.semaphore_signal(
            barrier, inc=1, device_id=(peer_s, peer_r, me_p), device_id_type=MESH
        )
        return carry

    lax.fori_loop(0, groups - 1, greet, 0)
    for off in range(1, tps):
        pl.semaphore_signal(
            barrier,
            inc=1,
            device_id=(me_s, me_r, lax.rem(me_p + off, tps)),
            device_id_type=MESH,
        )

    y0 = me_y * per_owner
    col0 = pl.multiple_of(me_c * half, LANES)
    loads = {}
    for place, (name, src, dst) in enumerate(
        (
            ("dgv", dgv_hbm, dgv),
            ("sq", sq_hbm, sq),
            ("dg", dg_hbm, dg_s),
            ("len", len_hbm, len_s),
            ("gate", gate_hbm, gate),
            ("pk", pk_hbm, pk),
            ("pv", pv_hbm, pv),
            ("pq", pq_hbm, pq),
            ("fq", fq_hbm, fq),
            ("fk", fk_hbm, fk),
            ("fv", fv_hbm, fv),
            ("sk", sk_hbm, sk),
            ("sv", sv_hbm, sv),
            ("sg", sg_hbm, sg),
            ("w", w_hbm, w),
            ("ck", ck_hbm, ck),
            ("cv", cv_hbm, cv),
            ("si", si_hbm.at[pl.ds(y0, per_owner), :, pl.ds(col0, half)], si),
            ("gain", gain_hbm.at[:, pl.ds(col0, half)], gain),
        )
    ):
        loads[name] = pltpu.make_async_copy(src, dst, in_sem.at[place])
        loads[name].start()

    loads["dgv"].wait()
    mine = dgv[...] == me_g
    mine_rows = jnp.broadcast_to(one_hot(mine), (16, total))
    before = one_hot(iota((total, total), 0) < iota((total, total), 1))
    rank = dot(mine_rows, before)[0:1]
    slot_row = lax.rem(iota((soft_rows * held, total), 0), held).astype(F32)
    slot_of = one_hot(jnp.where(mine, rank, -1.0) == slot_row)
    slot_lin = slot_of[: lin_rows * held]

    def rep_rows(rows_each):
        shape = (rows_each * reps, total)
        source_rep = lax.rem(iota(shape, 1) // held, reps)
        return one_hot(iota(shape, 0) // rows_each == source_rep)

    def spread(rows_each, slots):
        picked = dot_nt(rep_rows(rows_each), slots)
        same = lax.rem(iota(picked.shape, 0), rows_each) == iota(picked.shape, 1) // held
        return jnp.where(same, picked, 0.0).astype(BF16)

    def by_row(ref, count):
        pieces = [
            ref[i, :, a * LANES : (a + 1) * LANES].astype(F32)
            for a in range(count)
            for i in range(steps)
        ]
        return jnp.concatenate(pieces, axis=0).astype(BF16)

    loads["sq"].wait()
    spread_lin = spread(lin_rows, slot_lin)
    blocks = dot(spread_lin, by_row(sq, heads)).astype(BF16)
    send_q[...] = blocks.reshape(reps, lin_rows, LANES)

    for name in ("fq", "fk", "fv"):
        loads[name].wait()
    soft_blocks = dot(spread(soft_rows, slot_of), by_row(fq, q_heads)).astype(BF16)
    send_s[:, :soft_rows, :] = soft_blocks.reshape(reps, soft_rows, LANES)
    fresh = jnp.concatenate([by_row(fk, 1).astype(F32), by_row(fv, 1).astype(F32)], axis=0)
    fresh_spread = spread_lin[:, : 2 * steps * held]
    fresh_blocks = dot(fresh_spread, fresh.astype(BF16)).astype(BF16)
    send_s[:, soft_rows:, :] = fresh_blocks.reshape(reps, lin_rows, LANES)

    pl.semaphore_wait(barrier, groups - 1 + tps - 1)

    def to_groups(src, dst, sems):
        def one(m, carry):
            peer_s, peer_r = far_first(m)
            pltpu.make_async_remote_copy(
                src_ref=src.at[peer_r],
                dst_ref=dst.at[me_g],
                send_sem=sems.at[0],
                recv_sem=sems.at[1],
                device_id=(peer_s, peer_r, me_p),
                device_id_type=MESH,
            ).start()
            return carry

        lax.fori_loop(0, groups - 1, one, 0)
        dst[me_g] = src[me_r]

    def all_bytes(dst, sem):
        view = dst.at[pl.ds(0, dst.shape[0] - 1)]
        pltpu.make_async_copy(view, view, sem).wait()

    def rep_copy(off):
        peer_r = lax.rem(me_r + off, reps)
        return pltpu.make_async_remote_copy(
            src_ref=send_s.at[peer_r],
            dst_ref=recv_a.at[me_r],
            send_sem=a_sem.at[0],
            recv_sem=a_sem.at[1],
            device_id=(me_s, peer_r, me_p),
            device_id_type=MESH,
        )

    def section_copy(off):
        peer_s = lax.rem(me_s + off, sections)
        return pltpu.make_async_remote_copy(
            src_ref=send_b.at[peer_s],
            dst_ref=recv_b.at[me_s],
            send_sem=b_sem.at[0],
            recv_sem=b_sem.at[1],
            device_id=(peer_s, me_r, me_p),
            device_id_type=MESH,
        )

    to_groups(send_q, recv_q, q_sem)
    for off in range(1, reps):
        rep_copy(off).start()
    recv_a[me_r] = send_s[me_r]

    loads["dg"].wait()
    loads["len"].wait()
    loads["gate"].wait()
    count = held * heads
    shape = (count, length)
    own_len = [len_s[first + k] for k in range(held)]
    logs = jnp.log(jnp.concatenate([gate[k] for k in range(held)], axis=0))
    len_rows = jnp.zeros(shape, jnp.int32)
    for k in range(held):
        len_rows = jnp.where(iota(shape, 0) // heads == k, own_len[k], len_rows)
    inside = iota(shape, 1) < len_rows
    logs = jnp.where(inside, logs, 0.0)
    p1, rest = split_two(logs)
    rest = logs - p1.astype(F32)
    p2, p3 = split_two(rest)
    upto = one_hot(iota((length, length), 0) <= iota((length, length), 1))
    upto_t = one_hot(iota((length, length), 1) <= iota((length, length), 0))
    cum_rows = (dot(p1, upto) + dot(p2, upto) + dot(p3, upto)) * LOG2E
    cum_cols = (dot_nt(upto_t, p1) + dot_nt(upto_t, p2) + dot_nt(upto_t, p3)) * LOG2E
    shape = (length, count)
    len_cols = jnp.zeros(shape, jnp.int32)
    for k in range(held):
        len_cols = jnp.where(iota(shape, 1) // heads == k, own_len[k], len_cols)
    inside_cols = iota(shape, 0) < len_cols
    decays = jnp.where(inside_cols, jnp.exp2(cum_cols[length - 1 :] - cum_cols), 0.0)
    cum_cols = jnp.where(inside_cols, cum_cols, -jnp.inf)
    for k in range(held):
        rows = slice(k * heads, (k + 1) * heads)
        rowf[k] = cum_rows[rows]
        colm[k] = cum_cols[:, rows]
        colw[k] = decays[:, rows]

    loads["pk"].wait()
    loads["pv"].wait()

    def remember(k, carry):
        for h in range(heads):
            lanes = slice(h * LANES, (h + 1) * LANES)
            high, low = split_two(pv[k, :, lanes].astype(F32) * colw[k, :, h : h + 1])
            both = lax.dot_general(
                pk[k, :, lanes],
                jnp.concatenate([high, low], axis=1),
                (((0,), (0,)), ((), ())),
                preferred_element_type=F32,
            )
            high, low = split_two(both[:, :LANES] + both[:, LANES:])
            state[k, h, :LANES, :] = high
            state[k, h, LANES:, :] = low
        return carry

    lax.fori_loop(0, held, remember, 0)

    loads["pq"].wait()
    mid = length // 2

    def prompt(k, carry):
        causal = iota((mid, mid), 0) >= iota((mid, mid), 1)
        for h in range(heads):
            lanes = slice(h * LANES, (h + 1) * LANES)
            scores = dot_nt(pq[k, :, lanes], pk[k, :, lanes])
            row = rowf[k, h : h + 1, :]
            col = colm[k, :, h : h + 1]
            values = pv[k, :, lanes]
            gap = jnp.where(causal, col[:mid] - row[:, :mid], -jnp.inf)
            top = (jnp.exp2(gap) * scores[:mid, :mid]).astype(BF16)
            low_left = (jnp.exp2(col[mid:] - row[:, :mid]) * scores[mid:, :mid]).astype(BF16)
            gap = jnp.where(causal, col[mid:] - row[:, mid:], -jnp.inf)
            low_right = (jnp.exp2(gap) * scores[mid:, mid:]).astype(BF16)
            low = jnp.concatenate([low_left, low_right], axis=1)
            po[k, :mid, lanes] = dot(top, values[:mid]).astype(BF16)
            po[k, mid:, lanes] = dot(low, values).astype(BF16)
        return carry

    for name in ("sk", "sv", "sg"):
        loads[name].wait()
    eye = jnp.where(iota((held, held), 0) == iota((held, held), 1), 1.0, 0.0)
    gates = [dot_nt(eye, sg[i], lax.Precision.HIGHEST) for i in range(steps)]
    for h in range(heads):
        lanes = slice(h * LANES, (h + 1) * LANES)
        running = jnp.ones((held, 1), F32)
        for i in range(steps):
            running = running * gates[i][:, h : h + 1]
            gamma[i, :, lanes] = jnp.broadcast_to(running, (held, LANES))
            query = sq[i, :, lanes].astype(F32)
            added = jnp.zeros((held, LANES), F32)
            since = jnp.ones((held, 1), F32)
            for u in range(i, -1, -1):
                pair = jnp.sum(query * sk[u, :, lanes].astype(F32), axis=1, keepdims=True)
                added = added + (since * pair) * sv[u, :, lanes].astype(F32)
                since = since * gates[u][:, h : h + 1]
            own[i, :, lanes] = added

    def pick(rows_each, slots):
        shape = (total, rows_each * groups)
        source = one_hot(iota(shape, 0) // held == iota(shape, 1) // rows_each)
        picked = dot(slots, source)
        same = iota(picked.shape, 0) // held == lax.rem(iota(picked.shape, 1), rows_each)
        return jnp.where(same, picked, 0.0).astype(BF16)

    sel_lin[...] = pick(lin_rows, slot_lin)
    target_rep = [lax.rem(dg_s[first + k], reps) for k in range(held)]
    bound_for = []
    for r in range(reps):
        found = jnp.int32(0)
        for k in range(held):
            found = jnp.where(target_rep[k] == r, k, found)
        bound_for.append(found)
    each = held // sections
    onward = []
    for s in range(sections):
        chosen = [jnp.int32(0)] * each
        seen = jnp.int32(0)
        for k in range(held):
            group = dg_s[(s * reps + me_r) * held + k]
            hit = lax.div(group, reps) == me_s
            for c in range(each):
                chosen[c] = jnp.where(hit & (seen == c), lax.rem(group, reps), chosen[c])
            seen = seen + jnp.where(hit, 1, 0)
        onward.append(chosen)
    all_bytes(recv_q, q_sem.at[1])
    head_of_row = iota((lin_rows, LANES), 0) // steps
    for k in range(held):
        asked = recv_q[dg_s[first + k]].astype(F32)
        apart = []
        for h in range(heads):
            apart += [jnp.where(head_of_row == h, asked, 0.0).astype(BF16)] * 2
        states = state[k].reshape(2 * heads * LANES, LANES)
        res_q[k] = dot(jnp.concatenate(apart, axis=1), states).astype(BF16)
    for r in range(reps):
        send_r[r] = res_q[bound_for[r]]
    to_groups(send_r, recv_r, r_sem)

    all_bytes(recv_a, a_sem.at[1])
    for s in range(sections):
        for c in range(each):
            send_b[s, c] = recv_a[onward[s][c]]
    for off in range(1, sections):
        section_copy(off).start()
    recv_b[me_s] = send_b[me_s]

    sel_soft[...] = pick(soft_rows, slot_of)
    early = held // 2
    lax.fori_loop(0, early, prompt, 0)

    loads["w"].wait()
    all_bytes(recv_r, r_sem.at[1])
    carried = dot(sel_lin[...], recv_r[...].reshape(groups * lin_rows, LANES))
    hidden = []
    for i in range(steps):
        over_heads = []
        for h in range(heads):
            lanes = slice(h * LANES, (h + 1) * LANES)
            rows = slice((h * steps + i) * held, (h * steps + i + 1) * held)
            over_heads.append(gamma[i, :, lanes] * carried[rows] + own[i, :, lanes])
        hidden.append(jnp.concatenate(over_heads, axis=1))
    hidden = jnp.concatenate(hidden, axis=0).astype(BF16)
    wide = half // 2
    other0 = pl.multiple_of((1 - me_c) * half, LANES)

    by_distance = sorted(range(1, owners), key=lambda o: -min(o, owners - o))

    def sum_copy(which, q, off):
        owner = along_y(off)
        core = me_c if which else 1 - me_c
        return pltpu.make_async_remote_copy(
            src_ref=part_b.at[which, q, pl.ds(owner * per_owner, per_owner)],
            dst_ref=recv_p.at[me_p, q],
            send_sem=rs_send.at[owner, which, q],
            recv_sem=rs_recv.at[me_p, q],
            device_id=(me_s, me_r, owner * 2 + core),
            device_id_type=MESH,
        )

    def sum_copies(which):
        return by_distance if which else by_distance + [0]

    for which in range(2):
        start = col0 if which else other0
        for q in range(2):
            cols = pl.ds(pl.multiple_of(start + q * wide, LANES), wide)
            partial = dot(hidden, w[:, cols])
            for i in range(steps):
                rows = partial[i * held : (i + 1) * held]
                part_b[which, q, i] = rows.astype(BF16)
                if which:
                    part_f[q, i] = rows
            for off in sum_copies(which):
                sum_copy(which, q, off).start()

    loads["ck"].wait()
    loads["cv"].wait()
    all_bytes(recv_b, b_sem.at[1])
    scale = LOG2E / math.sqrt(LANES)

    def soft(k, carry):
        section = lax.div(dg_s[first + k], reps)
        place_of = jnp.int32(0)
        for k2 in range(held):
            same = (lax.div(dg_s[first + k2], reps) == section) & (k2 < k)
            place_of = place_of + jnp.where(same, 1, 0)
        block = recv_b[section, jnp.minimum(place_of, each - 1)]
        asked = block[:soft_rows]
        fresh_rows = block[soft_rows:]
        scores = dot_nt(asked, ck[k]) * scale
        scores = jnp.where(iota(scores.shape, 1) < len_s[first + k], scores, -jnp.inf)
        news = dot_nt(asked, fresh_rows) * scale
        lane = iota(news.shape, 1)
        seen = (lane < steps) & (lane <= lax.rem(iota(news.shape, 0), steps))
        news = jnp.where(seen, news, -jnp.inf)
        peak = jnp.maximum(
            jnp.max(scores, axis=1, keepdims=True), jnp.max(news, axis=1, keepdims=True)
        )
        scores = jnp.exp2(scores - peak)
        news = jnp.exp2(news - peak)
        bottom = jnp.sum(scores, axis=1, keepdims=True) + jnp.sum(news, axis=1, keepdims=True)
        probs = (scores / bottom).astype(BF16)
        fresh_probs = (news / bottom).astype(BF16).astype(F32)
        fresh_values = fresh_rows.astype(F32)
        mixed = dot(probs, cv[k])
        for u in range(steps):
            mixed = mixed + fresh_probs[:, u : u + 1] * fresh_values[steps + u : steps + u + 1]
        res_s[k] = mixed.astype(BF16)
        return carry

    lax.fori_loop(0, held, soft, 0)
    for r in range(reps):
        send_t[r] = res_s[bound_for[r]]
    to_groups(send_t, recv_t, t_sem)
    loads["si"].wait()
    loads["gain"].wait()
    summed = []
    for part in range(2):
        here = slice(part * wide, (part + 1) * wide)
        value = part_f[part, pl.ds(y0, per_owner)] + si[:, :, here].astype(F32)
        sources = [me_p + 1 - 2 * me_c]
        for off in reversed(by_distance):
            sources += [along_y(off) * 2, along_y(off) * 2 + 1]
        for source in sources:
            pltpu.make_async_copy(
                recv_p.at[source, part], recv_p.at[source, part], rs_recv.at[source, part]
            ).wait()
            value = value + recv_p[source, part].astype(F32)
        summed.append(value)
    square = jnp.sum(summed[0] * summed[0], axis=2, keepdims=True)
    square = square + jnp.sum(summed[1] * summed[1], axis=2, keepdims=True)
    ss_send[...] = jnp.broadcast_to(square, ss_send.shape)
    squares = pltpu.make_async_remote_copy(
        src_ref=ss_send,
        dst_ref=ss_recv,
        send_sem=ss_sem.at[0],
        recv_sem=ss_sem.at[1],
        device_id=sibling,
        device_id_type=MESH,
    )
    squares.start()
    squares.wait()
    mean = (square + ss_recv[:, :, 0:1]) / model
    spread_of = jnp.sqrt(mean + 1e-06)
    for part in range(2):
        here = slice(part * wide, (part + 1) * wide)
        cols = pl.ds(pl.multiple_of(col0 + part * wide, LANES), wide)
        gains = gain[:, here].reshape(1, 1, wide)
        do[pl.ds(y0, per_owner), :, cols] = (summed[part] / spread_of * gains).astype(BF16)

    def place(y):
        return do.at[pl.ds(y * per_owner, per_owner), :, pl.ds(col0, half)]

    def gather_copy(off):
        peer = along_y(off)
        return pltpu.make_async_remote_copy(
            src_ref=place(me_y),
            dst_ref=place(me_y),
            send_sem=ag_send.at[peer],
            recv_sem=ag_recv.at[me_y],
            device_id=(me_s, me_r, peer * 2 + me_c),
            device_id_type=MESH,
        )

    def pass_copy(y):
        return pltpu.make_async_remote_copy(
            src_ref=place(y),
            dst_ref=place(y),
            send_sem=pass_send.at[y],
            recv_sem=pass_recv.at[y],
            device_id=sibling,
            device_id_type=MESH,
        )

    for off in by_distance:
        gather_copy(off).start()
    pass_copy(me_y).start()

    lax.fori_loop(early, held, prompt, 0)

    all_bytes(recv_t, t_sem.at[1])
    placed = dot(sel_soft[...], recv_t[...].reshape(groups * soft_rows, LANES))
    for a in range(q_heads):
        for i in range(steps):
            rows = slice((a * steps + i) * held, (a * steps + i + 1) * held)
            so[i, :, a * LANES : (a + 1) * LANES] = placed[rows].astype(BF16)

    for off in reversed(by_distance):
        source = along_y(off)
        pltpu.make_async_copy(place(source), place(source), ag_recv.at[source]).wait()
        pass_copy(source).start()

    all_bytes(recv_q, q_sem.at[0])
    all_bytes(recv_r, r_sem.at[0])
    all_bytes(recv_a, a_sem.at[0])
    all_bytes(recv_b, b_sem.at[0])
    all_bytes(recv_t, t_sem.at[0])
    for which in range(2):
        for q in range(2):
            for off in sum_copies(which):
                sum_copy(which, q, off).wait_send()
    for off in range(1, owners):
        gather_copy(off).wait_send()
    for y in range(owners):
        pass_copy(y).wait()


def write_out(po, do, so, po_hbm, do_hbm, so_hbm, sem):
    held = po.shape[0]
    copies = [pltpu.make_async_copy(po.at[k], po_hbm.at[k], sem.at[k]) for k in range(held)]
    copies.append(pltpu.make_async_copy(do, do_hbm, sem.at[held]))
    copies.append(pltpu.make_async_copy(so, so_hbm, sem.at[held + 1]))
    for copy in copies:
        copy.start()
    for copy in copies:
        copy.wait()


def on_device(
    prefill_query,
    prefill_key,
    prefill_value,
    prefill_gate,
    lengths,
    decode_group,
    cache_keys,
    cache_values,
    out_weight,
    norm_gain,
    step_input,
    step_query,
    step_key,
    step_value,
    step_gate,
    soft_query,
    soft_new_key,
    soft_new_value,
):
    sections, reps, tps = (lax.axis_size(name) for name in ("section", "rep", "tp"))
    held, length, heads = prefill_gate.shape
    steps = step_query.shape[0]
    q_heads = soft_query.shape[2] // LANES
    model = out_weight.shape[1]
    groups = sections * reps
    width = heads * LANES
    half = model // 2
    per_owner = steps * 2 // tps
    lin_rows = heads * steps
    soft_rows = q_heads * steps
    total = groups * held
    dims = (sections, reps, tps, held, length, heads, steps, q_heads, model)
    operands = (
        prefill_query,
        prefill_key,
        prefill_value,
        jnp.transpose(prefill_gate, (0, 2, 1)),
        lengths,
        decode_group,
        decode_group.reshape(1, total),
        cache_keys,
        cache_values,
        out_weight,
        norm_gain.reshape(1, model),
        step_input,
        step_query,
        step_key,
        step_value,
        jnp.transpose(step_gate, (0, 2, 1)),
        soft_query,
        soft_new_key,
        soft_new_value,
    )
    vmem = pltpu.VMEM
    dma = pltpu.SemaphoreType.DMA
    scratch = [
        vmem((held, length, width), BF16),
        vmem((held, length, width), BF16),
        vmem((held, length, width), BF16),
        vmem((held, heads, length), F32),
        pltpu.SMEM((total,), jnp.int32),
        pltpu.SMEM((total,), jnp.int32),
        vmem((1, total), jnp.int32),
        vmem((held, length, LANES), BF16),
        vmem((held, length, LANES), BF16),
        vmem((width, model), BF16),
        vmem((1, half), F32),
        vmem((per_owner, held, half), BF16),
        vmem((steps, held, width), BF16),
        vmem((steps, held, width), BF16),
        vmem((steps, held, width), BF16),
        vmem((steps, heads, held), F32),
        vmem((steps, held, q_heads * LANES), BF16),
        vmem((steps, held, LANES), BF16),
        vmem((steps, held, LANES), BF16),
        vmem((held, heads, length), F32),
        vmem((held, length, heads), F32),
        vmem((held, length, heads), F32),
        vmem((held, heads, 2 * LANES, LANES), BF16),
        vmem((steps, held, width), F32),
        vmem((steps, held, width), F32),
        vmem((lin_rows * held, lin_rows * groups), BF16),
        vmem((soft_rows * held, soft_rows * groups), BF16),
        vmem((reps, lin_rows, LANES), BF16),
        vmem((groups, lin_rows, LANES), BF16),
        vmem((held, lin_rows, LANES), BF16),
        vmem((reps, lin_rows, LANES), BF16),
        vmem((groups, lin_rows, LANES), BF16),
        vmem((reps, soft_rows + lin_rows, LANES), BF16),
        vmem((reps, soft_rows + lin_rows, LANES), BF16),
        vmem((sections, held // sections, soft_rows + lin_rows, LANES), BF16),
        vmem((sections, held // sections, soft_rows + lin_rows, LANES), BF16),
        vmem((held, soft_rows, LANES), BF16),
        vmem((reps, soft_rows, LANES), BF16),
        vmem((groups, soft_rows, LANES), BF16),
        vmem((2, steps, held, half // 2), F32),
        vmem((2, 2, steps, held, half // 2), BF16),
        vmem((tps, 2, per_owner, held, half // 2), BF16),
        vmem((per_owner, held, LANES), F32),
        vmem((per_owner, held, LANES), F32),
        dma((19,)),
        dma((2,)),
        dma((2,)),
        dma((2,)),
        dma((2,)),
        dma((2,)),
        dma((tps // 2, 2, 2)),
        dma((tps, 2)),
        dma((2,)),
        dma((tps // 2,)),
        dma((tps // 2,)),
        dma((tps // 2,)),
        dma((tps // 2,)),
    ]
    anywhere = pl.BlockSpec(memory_space=pl.ANY)
    results = pl.pallas_call(
        functools.partial(body, dims),
        out_shape=(
            vmem((held, length, width), BF16),
            vmem((steps, held, model), BF16),
            vmem((steps, held, q_heads * LANES), BF16),
        ),
        in_specs=[anywhere] * len(operands),
        out_specs=(pl.BlockSpec(memory_space=vmem),) * 3,
        scratch_shapes=scratch,
        compiler_params=pltpu.CompilerParams(
            collective_id=0, has_side_effects=True, vmem_limit_bytes=56 * 1024 * 1024
        ),
    )(*operands)
    results = [pltpu.with_memory_space_constraint(x, pltpu.VMEM) for x in results]
    return pl.pallas_call(
        write_out,
        out_shape=[jax.ShapeDtypeStruct(array.shape, array.dtype) for array in results],
        in_specs=[anywhere] * 3,
        out_specs=[anywhere] * 3,
        scratch_shapes=[dma((held + 2,))],
    )(*results)


def solution(mesh):
    rows = P(("section", "rep"), None, "tp")
    slots = P(None, ("section", "rep"), "tp")
    whole = P(None, ("section", "rep"), None)
    return jax.shard_map(
        on_device,
        mesh=mesh,
        in_specs=(
            rows,
            rows,
            rows,
            rows,
            P(),
            P(),
            rows,
            rows,
            P("tp", None),
            P(),
            whole,
            slots,
            slots,
            slots,
            slots,
            slots,
            slots,
            slots,
        ),
        out_specs=(rows, whole, slots),
        check_vma=False,
    )
```

```python
import functools
import math

import jax
import jax.numpy as jnp
from jax import lax
from jax.experimental import pallas as pl
from jax.experimental.pallas import tpu as pltpu
from jax.sharding import PartitionSpec as P

MESH = pl.DeviceIdType.MESH
F32 = jnp.float32
BF16 = jnp.bfloat16
LOG2E = 1.0 / math.log(2.0)
LANES = 128


def iota(shape, axis):
    return lax.broadcasted_iota(jnp.int32, shape, axis)


def dot(a, b):
    return jnp.dot(a, b, preferred_element_type=F32)


def dot_nt(a, b, precision=None):
    return lax.dot_general(
        a, b, (((1,), (1,)), ((), ())), preferred_element_type=F32, precision=precision
    )


def one_hot(mask):
    return jnp.where(mask, 1.0, 0.0).astype(BF16)


def split_two(x):
    high = x.astype(BF16)
    return high, (x - high.astype(F32)).astype(BF16)


def body(
    dims,
    pq_hbm,
    pk_hbm,
    pv_hbm,
    gate_hbm,
    len_hbm,
    dg_hbm,
    dgv_hbm,
    ck_hbm,
    cv_hbm,
    w_hbm,
    gain_hbm,
    si_hbm,
    sq_hbm,
    sk_hbm,
    sv_hbm,
    sg_hbm,
    fq_hbm,
    fk_hbm,
    fv_hbm,
    po,
    do,
    so,
    pq,
    pk,
    pv,
    gate,
    len_s,
    dg_s,
    dgv,
    ck,
    cv,
    w,
    gain,
    si,
    sq,
    sk,
    sv,
    sg,
    fq,
    fk,
    fv,
    rowf,
    colm,
    colw,
    state,
    own,
    gamma,
    sel_lin,
    sel_soft,
    send_q,
    recv_q,
    res_q,
    send_r,
    recv_r,
    send_s,
    recv_a,
    send_b,
    recv_b,
    res_s,
    send_t,
    recv_t,
    part_f,
    part_b,
    recv_p,
    ss_send,
    ss_recv,
    in_sem,
    q_sem,
    r_sem,
    a_sem,
    b_sem,
    t_sem,
    rs_send,
    rs_recv,
    ss_sem,
    ag_send,
    ag_recv,
    pass_send,
    pass_recv,
):
    sections, reps, tps, held, length, heads, steps, q_heads, model = dims
    groups = sections * reps
    total = groups * held
    me_s = lax.axis_index("section")
    me_r = lax.axis_index("rep")
    me_p = lax.axis_index("tp")
    me_g = me_s * reps + me_r
    first = me_g * held
    half = model // 2
    per_owner = steps * 2 // tps
    me_y = me_p // 2
    me_c = me_p % 2
    lin_rows = heads * steps
    soft_rows = q_heads * steps

    owners = tps // 2
    sibling = (me_s, me_r, me_p + 1 - 2 * me_c)

    deep = 2 * sections
    across = reps // 2
    me_z = (me_r // across) * sections + me_s
    me_x = lax.rem(me_r, across)

    def ring(me, size):
        return {d: lax.rem(me + d, size) for d in range(size)}

    def hops(d, size):
        return min(d, size - d)

    z_at = ring(me_z, deep)
    x_at = ring(me_x, across)
    section_at = {d: lax.rem(z, sections) for d, z in z_at.items()}
    rep_at = {d: lax.div(z, sections) * across for d, z in z_at.items()}
    far_first = sorted(
        ((dz, dx) for dz in range(deep) for dx in range(across) if dz or dx),
        key=lambda d: -hops(d[0], deep) - hops(d[1], across),
    )
    y_at = ring(me_y, owners)

    def along_y(off):
        return y_at[off]

    barrier = pltpu.get_barrier_semaphore()

    for dz, dx in far_first:
        pl.semaphore_signal(
            barrier,
            inc=1,
            device_id=(section_at[dz], rep_at[dz] + x_at[dx], me_p),
            device_id_type=MESH,
        )
    for off in range(1, tps):
        pl.semaphore_signal(
            barrier,
            inc=1,
            device_id=(me_s, me_r, lax.rem(me_p + off, tps)),
            device_id_type=MESH,
        )

    y0 = me_y * per_owner
    col0 = pl.multiple_of(me_c * half, LANES)
    loads = {}
    for place, (name, src, dst) in enumerate(
        (
            ("dgv", dgv_hbm, dgv),
            ("sq", sq_hbm, sq),
            ("dg", dg_hbm, dg_s),
            ("len", len_hbm, len_s),
            ("gate", gate_hbm, gate),
            ("pk", pk_hbm, pk),
            ("pv", pv_hbm, pv),
            ("pq", pq_hbm, pq),
            ("fq", fq_hbm, fq),
            ("fk", fk_hbm, fk),
            ("fv", fv_hbm, fv),
            ("sk", sk_hbm, sk),
            ("sv", sv_hbm, sv),
            ("sg", sg_hbm, sg),
            ("w", w_hbm, w),
            ("ck", ck_hbm, ck),
            ("cv", cv_hbm, cv),
            ("si", si_hbm.at[pl.ds(y0, per_owner), :, pl.ds(col0, half)], si),
            ("gain", gain_hbm.at[:, pl.ds(col0, half)], gain),
        )
    ):
        loads[name] = pltpu.make_async_copy(src, dst, in_sem.at[place])
        loads[name].start()

    loads["dgv"].wait()
    mine = dgv[...] == me_g
    mine_rows = jnp.broadcast_to(one_hot(mine), (16, total))
    before = one_hot(iota((total, total), 0) < iota((total, total), 1))
    rank = dot(mine_rows, before)[0:1]
    slot_row = lax.rem(iota((soft_rows * held, total), 0), held).astype(F32)
    slot_of = one_hot(jnp.where(mine, rank, -1.0) == slot_row)
    slot_lin = slot_of[: lin_rows * held]

    def rep_rows(rows_each):
        shape = (rows_each * reps, total)
        source_rep = lax.rem(iota(shape, 1) // held, reps)
        return one_hot(iota(shape, 0) // rows_each == source_rep)

    def spread(rows_each, slots):
        picked = dot_nt(rep_rows(rows_each), slots)
        same = lax.rem(iota(picked.shape, 0), rows_each) == iota(picked.shape, 1) // held
        return jnp.where(same, picked, 0.0).astype(BF16)

    def by_row(ref, count):
        pieces = [
            ref[i, :, a * LANES : (a + 1) * LANES].astype(F32)
            for a in range(count)
            for i in range(steps)
        ]
        return jnp.concatenate(pieces, axis=0).astype(BF16)

    loads["sq"].wait()
    spread_lin = spread(lin_rows, slot_lin)
    blocks = dot(spread_lin, by_row(sq, heads)).astype(BF16)
    send_q[...] = blocks.reshape(reps, lin_rows, LANES)

    for name in ("fq", "fk", "fv"):
        loads[name].wait()
    soft_blocks = dot(spread(soft_rows, slot_of), by_row(fq, q_heads)).astype(BF16)
    send_s[:, :soft_rows, :] = soft_blocks.reshape(reps, soft_rows, LANES)
    fresh = jnp.concatenate([by_row(fk, 1).astype(F32), by_row(fv, 1).astype(F32)], axis=0)
    fresh_spread = spread_lin[:, : 2 * steps * held]
    fresh_blocks = dot(fresh_spread, fresh.astype(BF16)).astype(BF16)
    send_s[:, soft_rows:, :] = fresh_blocks.reshape(reps, lin_rows, LANES)

    pl.semaphore_wait(barrier, groups - 1 + tps - 1)

    def to_groups(src, dst, sems):
        for dz, dx in far_first:
            peer_r = rep_at[dz] + x_at[dx]
            pltpu.make_async_remote_copy(
                src_ref=src.at[peer_r],
                dst_ref=dst.at[me_g],
                send_sem=sems.at[0],
                recv_sem=sems.at[1],
                device_id=(section_at[dz], peer_r, me_p),
                device_id_type=MESH,
            ).start()
        dst[me_g] = src[me_r]

    def all_bytes(dst, sem):
        view = dst.at[pl.ds(0, dst.shape[0] - 1)]
        pltpu.make_async_copy(view, view, sem).wait()

    def rep_copy(off):
        peer_r = lax.rem(me_r + off, reps)
        return pltpu.make_async_remote_copy(
            src_ref=send_s.at[peer_r],
            dst_ref=recv_a.at[me_r],
            send_sem=a_sem.at[0],
            recv_sem=a_sem.at[1],
            device_id=(me_s, peer_r, me_p),
            device_id_type=MESH,
        )

    def section_copy(off):
        peer_s = lax.rem(me_s + off, sections)
        return pltpu.make_async_remote_copy(
            src_ref=send_b.at[peer_s],
            dst_ref=recv_b.at[me_s],
            send_sem=b_sem.at[0],
            recv_sem=b_sem.at[1],
            device_id=(peer_s, me_r, me_p),
            device_id_type=MESH,
        )

    to_groups(send_q, recv_q, q_sem)
    for off in range(1, reps):
        rep_copy(off).start()
    recv_a[me_r] = send_s[me_r]

    loads["dg"].wait()
    loads["len"].wait()
    loads["gate"].wait()
    count = held * heads
    shape = (count, length)
    own_len = [len_s[first + k] for k in range(held)]
    logs = jnp.log(jnp.concatenate([gate[k] for k in range(held)], axis=0))
    len_rows = jnp.zeros(shape, jnp.int32)
    for k in range(held):
        len_rows = jnp.where(iota(shape, 0) // heads == k, own_len[k], len_rows)
    inside = iota(shape, 1) < len_rows
    logs = jnp.where(inside, logs, 0.0)
    p1, rest = split_two(logs)
    rest = logs - p1.astype(F32)
    p2, p3 = split_two(rest)
    upto = one_hot(iota((length, length), 0) <= iota((length, length), 1))
    upto_t = one_hot(iota((length, length), 1) <= iota((length, length), 0))
    cum_rows = (dot(p1, upto) + dot(p2, upto) + dot(p3, upto)) * LOG2E
    cum_cols = (dot_nt(upto_t, p1) + dot_nt(upto_t, p2) + dot_nt(upto_t, p3)) * LOG2E
    shape = (length, count)
    len_cols = jnp.zeros(shape, jnp.int32)
    for k in range(held):
        len_cols = jnp.where(iota(shape, 1) // heads == k, own_len[k], len_cols)
    inside_cols = iota(shape, 0) < len_cols
    decays = jnp.where(inside_cols, jnp.exp2(cum_cols[length - 1 :] - cum_cols), 0.0)
    cum_cols = jnp.where(inside_cols, cum_cols, -jnp.inf)
    for k in range(held):
        rows = slice(k * heads, (k + 1) * heads)
        rowf[k] = cum_rows[rows]
        colm[k] = cum_cols[:, rows]
        colw[k] = decays[:, rows]

    loads["pk"].wait()
    loads["pv"].wait()

    def remember(k, carry):
        for h in range(heads):
            lanes = slice(h * LANES, (h + 1) * LANES)
            high, low = split_two(pv[k, :, lanes].astype(F32) * colw[k, :, h : h + 1])
            both = lax.dot_general(
                pk[k, :, lanes],
                jnp.concatenate([high, low], axis=1),
                (((0,), (0,)), ((), ())),
                preferred_element_type=F32,
            )
            high, low = split_two(both[:, :LANES] + both[:, LANES:])
            state[k, h, :LANES, :] = high
            state[k, h, LANES:, :] = low
        return carry

    lax.fori_loop(0, held, remember, 0)

    loads["pq"].wait()
    mid = length // 2

    def prompt(k, carry):
        causal = iota((mid, mid), 0) >= iota((mid, mid), 1)
        for h in range(heads):
            lanes = slice(h * LANES, (h + 1) * LANES)
            scores = dot_nt(pq[k, :, lanes], pk[k, :, lanes])
            row = rowf[k, h : h + 1, :]
            col = colm[k, :, h : h + 1]
            values = pv[k, :, lanes]
            gap = jnp.where(causal, col[:mid] - row[:, :mid], -jnp.inf)
            top = (jnp.exp2(gap) * scores[:mid, :mid]).astype(BF16)
            low_left = (jnp.exp2(col[mid:] - row[:, :mid]) * scores[mid:, :mid]).astype(BF16)
            gap = jnp.where(causal, col[mid:] - row[:, mid:], -jnp.inf)
            low_right = (jnp.exp2(gap) * scores[mid:, mid:]).astype(BF16)
            low = jnp.concatenate([low_left, low_right], axis=1)
            po[k, :mid, lanes] = dot(top, values[:mid]).astype(BF16)
            po[k, mid:, lanes] = dot(low, values).astype(BF16)
        return carry

    for name in ("sk", "sv", "sg"):
        loads[name].wait()
    eye = jnp.where(iota((held, held), 0) == iota((held, held), 1), 1.0, 0.0)
    gates = [dot_nt(eye, sg[i], lax.Precision.HIGHEST) for i in range(steps)]
    for h in range(heads):
        lanes = slice(h * LANES, (h + 1) * LANES)
        running = jnp.ones((held, 1), F32)
        for i in range(steps):
            running = running * gates[i][:, h : h + 1]
            gamma[i, :, lanes] = jnp.broadcast_to(running, (held, LANES))
            query = sq[i, :, lanes].astype(F32)
            added = jnp.zeros((held, LANES), F32)
            since = jnp.ones((held, 1), F32)
            for u in range(i, -1, -1):
                pair = jnp.sum(query * sk[u, :, lanes].astype(F32), axis=1, keepdims=True)
                added = added + (since * pair) * sv[u, :, lanes].astype(F32)
                since = since * gates[u][:, h : h + 1]
            own[i, :, lanes] = added

    def pick(rows_each, slots):
        shape = (total, rows_each * groups)
        source = one_hot(iota(shape, 0) // held == iota(shape, 1) // rows_each)
        picked = dot(slots, source)
        same = iota(picked.shape, 0) // held == lax.rem(iota(picked.shape, 1), rows_each)
        return jnp.where(same, picked, 0.0).astype(BF16)

    sel_lin[...] = pick(lin_rows, slot_lin)
    target_rep = [lax.rem(dg_s[first + k], reps) for k in range(held)]
    bound_for = []
    for r in range(reps):
        found = jnp.int32(0)
        for k in range(held):
            found = jnp.where(target_rep[k] == r, k, found)
        bound_for.append(found)
    each = held // sections
    onward = []
    for s in range(sections):
        chosen = [jnp.int32(0)] * each
        seen = jnp.int32(0)
        for k in range(held):
            group = dg_s[(s * reps + me_r) * held + k]
            hit = lax.div(group, reps) == me_s
            for c in range(each):
                chosen[c] = jnp.where(hit & (seen == c), lax.rem(group, reps), chosen[c])
            seen = seen + jnp.where(hit, 1, 0)
        onward.append(chosen)
    all_bytes(recv_q, q_sem.at[1])
    head_of_row = iota((lin_rows, LANES), 0) // steps
    for k in range(held):
        asked = recv_q[dg_s[first + k]].astype(F32)
        apart = []
        for h in range(heads):
            apart += [jnp.where(head_of_row == h, asked, 0.0).astype(BF16)] * 2
        states = state[k].reshape(2 * heads * LANES, LANES)
        res_q[k] = dot(jnp.concatenate(apart, axis=1), states).astype(BF16)
    for r in range(reps):
        send_r[r] = res_q[bound_for[r]]
    to_groups(send_r, recv_r, r_sem)

    all_bytes(recv_a, a_sem.at[1])
    for s in range(sections):
        for c in range(each):
            send_b[s, c] = recv_a[onward[s][c]]
    for off in range(1, sections):
        section_copy(off).start()
    recv_b[me_s] = send_b[me_s]

    sel_soft[...] = pick(soft_rows, slot_of)
    early = held // 2
    lax.fori_loop(0, early, prompt, 0)

    loads["w"].wait()
    all_bytes(recv_r, r_sem.at[1])
    carried = dot(sel_lin[...], recv_r[...].reshape(groups * lin_rows, LANES))
    hidden = []
    for i in range(steps):
        over_heads = []
        for h in range(heads):
            lanes = slice(h * LANES, (h + 1) * LANES)
            rows = slice((h * steps + i) * held, (h * steps + i + 1) * held)
            over_heads.append(gamma[i, :, lanes] * carried[rows] + own[i, :, lanes])
        hidden.append(jnp.concatenate(over_heads, axis=1))
    hidden = jnp.concatenate(hidden, axis=0).astype(BF16)
    wide = half // 2
    other0 = pl.multiple_of((1 - me_c) * half, LANES)

    by_distance = sorted(range(1, owners), key=lambda o: -min(o, owners - o))

    def sum_copy(which, q, off):
        owner = along_y(off)
        core = me_c if which else 1 - me_c
        return pltpu.make_async_remote_copy(
            src_ref=part_b.at[which, q, pl.ds(owner * per_owner, per_owner)],
            dst_ref=recv_p.at[me_p, q],
            send_sem=rs_send.at[owner, which, q],
            recv_sem=rs_recv.at[me_p, q],
            device_id=(me_s, me_r, owner * 2 + core),
            device_id_type=MESH,
        )

    def sum_copies(which):
        return by_distance if which else by_distance + [0]

    for which in range(2):
        start = col0 if which else other0
        for q in range(2):
            cols = pl.ds(pl.multiple_of(start + q * wide, LANES), wide)
            partial = dot(hidden, w[:, cols])
            for i in range(steps):
                rows = partial[i * held : (i + 1) * held]
                part_b[which, q, i] = rows.astype(BF16)
                if which:
                    part_f[q, i] = rows
            for off in sum_copies(which):
                sum_copy(which, q, off).start()

    loads["ck"].wait()
    loads["cv"].wait()
    all_bytes(recv_b, b_sem.at[1])
    scale = LOG2E / math.sqrt(LANES)

    def soft(k, carry):
        section = lax.div(dg_s[first + k], reps)
        place_of = jnp.int32(0)
        for k2 in range(held):
            same = (lax.div(dg_s[first + k2], reps) == section) & (k2 < k)
            place_of = place_of + jnp.where(same, 1, 0)
        block = recv_b[section, jnp.minimum(place_of, each - 1)]
        asked = block[:soft_rows]
        fresh_rows = block[soft_rows:]
        scores = dot_nt(asked, ck[k]) * scale
        scores = jnp.where(iota(scores.shape, 1) < len_s[first + k], scores, -jnp.inf)
        news = dot_nt(asked, fresh_rows) * scale
        lane = iota(news.shape, 1)
        seen = (lane < steps) & (lane <= lax.rem(iota(news.shape, 0), steps))
        news = jnp.where(seen, news, -jnp.inf)
        peak = jnp.maximum(
            jnp.max(scores, axis=1, keepdims=True), jnp.max(news, axis=1, keepdims=True)
        )
        scores = jnp.exp2(scores - peak)
        news = jnp.exp2(news - peak)
        bottom = jnp.sum(scores, axis=1, keepdims=True) + jnp.sum(news, axis=1, keepdims=True)
        probs = (scores / bottom).astype(BF16)
        fresh_probs = (news / bottom).astype(BF16).astype(F32)
        fresh_values = fresh_rows.astype(F32)
        mixed = dot(probs, cv[k])
        for u in range(steps):
            mixed = mixed + fresh_probs[:, u : u + 1] * fresh_values[steps + u : steps + u + 1]
        res_s[k] = mixed.astype(BF16)
        return carry

    lax.fori_loop(0, held, soft, 0)
    for r in range(reps):
        send_t[r] = res_s[bound_for[r]]
    to_groups(send_t, recv_t, t_sem)
    loads["si"].wait()
    loads["gain"].wait()
    summed = []
    for part in range(2):
        here = slice(part * wide, (part + 1) * wide)
        value = part_f[part, pl.ds(y0, per_owner)] + si[:, :, here].astype(F32)
        sources = [me_p + 1 - 2 * me_c]
        for off in reversed(by_distance):
            sources += [along_y(off) * 2, along_y(off) * 2 + 1]
        for source in sources:
            pltpu.make_async_copy(
                recv_p.at[source, part], recv_p.at[source, part], rs_recv.at[source, part]
            ).wait()
            value = value + recv_p[source, part].astype(F32)
        summed.append(value)
    square = jnp.sum(summed[0] * summed[0], axis=2, keepdims=True)
    square = square + jnp.sum(summed[1] * summed[1], axis=2, keepdims=True)
    ss_send[...] = jnp.broadcast_to(square, ss_send.shape)
    squares = pltpu.make_async_remote_copy(
        src_ref=ss_send,
        dst_ref=ss_recv,
        send_sem=ss_sem.at[0],
        recv_sem=ss_sem.at[1],
        device_id=sibling,
        device_id_type=MESH,
    )
    squares.start()
    squares.wait()
    mean = (square + ss_recv[:, :, 0:1]) / model
    spread_of = jnp.sqrt(mean + 1e-06)
    def place(y, part):
        cols = pl.ds(pl.multiple_of(col0 + part * wide, LANES), wide)
        return do.at[pl.ds(y * per_owner, per_owner), :, cols]

    def gather_copy(off, part):
        peer = along_y(off)
        return pltpu.make_async_remote_copy(
            src_ref=place(me_y, part),
            dst_ref=place(me_y, part),
            send_sem=ag_send.at[peer, part],
            recv_sem=ag_recv.at[me_y, part],
            device_id=(me_s, me_r, peer * 2 + me_c),
            device_id_type=MESH,
        )

    def pass_copy(y, part):
        return pltpu.make_async_remote_copy(
            src_ref=place(y, part),
            dst_ref=place(y, part),
            send_sem=pass_send.at[y, part],
            recv_sem=pass_recv.at[y, part],
            device_id=sibling,
            device_id_type=MESH,
        )

    for part in range(2):
        here = slice(part * wide, (part + 1) * wide)
        gains = gain[:, here].reshape(1, 1, wide)
        place(me_y, part)[...] = (summed[part] / spread_of * gains).astype(BF16)
        for off in by_distance:
            gather_copy(off, part).start()
    for part in range(2):
        pass_copy(me_y, part).start()

    lax.fori_loop(early, held, prompt, 0)

    for part in range(2):
        for off in reversed(by_distance):
            source = along_y(off)
            landed = place(source, part)
            pltpu.make_async_copy(landed, landed, ag_recv.at[source, part]).wait()
            pass_copy(source, part).start()

    all_bytes(recv_t, t_sem.at[1])
    placed = dot(sel_soft[...], recv_t[...].reshape(groups * soft_rows, LANES))
    for a in range(q_heads):
        for i in range(steps):
            rows = slice((a * steps + i) * held, (a * steps + i + 1) * held)
            so[i, :, a * LANES : (a + 1) * LANES] = placed[rows].astype(BF16)

    all_bytes(recv_q, q_sem.at[0])
    all_bytes(recv_r, r_sem.at[0])
    all_bytes(recv_a, a_sem.at[0])
    all_bytes(recv_b, b_sem.at[0])
    all_bytes(recv_t, t_sem.at[0])
    for which in range(2):
        for q in range(2):
            for off in sum_copies(which):
                sum_copy(which, q, off).wait_send()
    for part in range(2):
        for off in range(1, owners):
            gather_copy(off, part).wait_send()
        for y in range(owners):
            pass_copy(y, part).wait()


def write_out(po, do, so, po_hbm, do_hbm, so_hbm, sem):
    held = po.shape[0]
    copies = [pltpu.make_async_copy(po.at[k], po_hbm.at[k], sem.at[k]) for k in range(held)]
    copies.append(pltpu.make_async_copy(do, do_hbm, sem.at[held]))
    copies.append(pltpu.make_async_copy(so, so_hbm, sem.at[held + 1]))
    for copy in copies:
        copy.start()
    for copy in copies:
        copy.wait()


def on_device(
    prefill_query,
    prefill_key,
    prefill_value,
    prefill_gate,
    lengths,
    decode_group,
    cache_keys,
    cache_values,
    out_weight,
    norm_gain,
    step_input,
    step_query,
    step_key,
    step_value,
    step_gate,
    soft_query,
    soft_new_key,
    soft_new_value,
):
    sections, reps, tps = (lax.axis_size(name) for name in ("section", "rep", "tp"))
    held, length, heads = prefill_gate.shape
    steps = step_query.shape[0]
    q_heads = soft_query.shape[2] // LANES
    model = out_weight.shape[1]
    groups = sections * reps
    width = heads * LANES
    half = model // 2
    per_owner = steps * 2 // tps
    lin_rows = heads * steps
    soft_rows = q_heads * steps
    total = groups * held
    dims = (sections, reps, tps, held, length, heads, steps, q_heads, model)
    operands = (
        prefill_query,
        prefill_key,
        prefill_value,
        jnp.transpose(prefill_gate, (0, 2, 1)),
        lengths,
        decode_group,
        decode_group.reshape(1, total),
        cache_keys,
        cache_values,
        out_weight,
        norm_gain.reshape(1, model),
        step_input,
        step_query,
        step_key,
        step_value,
        jnp.transpose(step_gate, (0, 2, 1)),
        soft_query,
        soft_new_key,
        soft_new_value,
    )
    vmem = pltpu.VMEM
    dma = pltpu.SemaphoreType.DMA
    scratch = [
        vmem((held, length, width), BF16),
        vmem((held, length, width), BF16),
        vmem((held, length, width), BF16),
        vmem((held, heads, length), F32),
        pltpu.SMEM((total,), jnp.int32),
        pltpu.SMEM((total,), jnp.int32),
        vmem((1, total), jnp.int32),
        vmem((held, length, LANES), BF16),
        vmem((held, length, LANES), BF16),
        vmem((width, model), BF16),
        vmem((1, half), F32),
        vmem((per_owner, held, half), BF16),
        vmem((steps, held, width), BF16),
        vmem((steps, held, width), BF16),
        vmem((steps, held, width), BF16),
        vmem((steps, heads, held), F32),
        vmem((steps, held, q_heads * LANES), BF16),
        vmem((steps, held, LANES), BF16),
        vmem((steps, held, LANES), BF16),
        vmem((held, heads, length), F32),
        vmem((held, length, heads), F32),
        vmem((held, length, heads), F32),
        vmem((held, heads, 2 * LANES, LANES), BF16),
        vmem((steps, held, width), F32),
        vmem((steps, held, width), F32),
        vmem((lin_rows * held, lin_rows * groups), BF16),
        vmem((soft_rows * held, soft_rows * groups), BF16),
        vmem((reps, lin_rows, LANES), BF16),
        vmem((groups, lin_rows, LANES), BF16),
        vmem((held, lin_rows, LANES), BF16),
        vmem((reps, lin_rows, LANES), BF16),
        vmem((groups, lin_rows, LANES), BF16),
        vmem((reps, soft_rows + lin_rows, LANES), BF16),
        vmem((reps, soft_rows + lin_rows, LANES), BF16),
        vmem((sections, held // sections, soft_rows + lin_rows, LANES), BF16),
        vmem((sections, held // sections, soft_rows + lin_rows, LANES), BF16),
        vmem((held, soft_rows, LANES), BF16),
        vmem((reps, soft_rows, LANES), BF16),
        vmem((groups, soft_rows, LANES), BF16),
        vmem((2, steps, held, half // 2), F32),
        vmem((2, 2, steps, held, half // 2), BF16),
        vmem((tps, 2, per_owner, held, half // 2), BF16),
        vmem((per_owner, held, LANES), F32),
        vmem((per_owner, held, LANES), F32),
        dma((19,)),
        dma((2,)),
        dma((2,)),
        dma((2,)),
        dma((2,)),
        dma((2,)),
        dma((tps // 2, 2, 2)),
        dma((tps, 2)),
        dma((2,)),
        dma((tps // 2, 2)),
        dma((tps // 2, 2)),
        dma((tps // 2, 2)),
        dma((tps // 2, 2)),
    ]
    anywhere = pl.BlockSpec(memory_space=pl.ANY)
    results = pl.pallas_call(
        functools.partial(body, dims),
        out_shape=(
            vmem((held, length, width), BF16),
            vmem((steps, held, model), BF16),
            vmem((steps, held, q_heads * LANES), BF16),
        ),
        in_specs=[anywhere] * len(operands),
        out_specs=(pl.BlockSpec(memory_space=vmem),) * 3,
        scratch_shapes=scratch,
        compiler_params=pltpu.CompilerParams(
            collective_id=0, has_side_effects=True, vmem_limit_bytes=56 * 1024 * 1024
        ),
    )(*operands)
    results = [pltpu.with_memory_space_constraint(x, pltpu.VMEM) for x in results]
    return pl.pallas_call(
        write_out,
        out_shape=[jax.ShapeDtypeStruct(array.shape, array.dtype) for array in results],
        in_specs=[anywhere] * 3,
        out_specs=[anywhere] * 3,
        scratch_shapes=[dma((held + 2,))],
    )(*results)


def solution(mesh):
    rows = P(("section", "rep"), None, "tp")
    slots = P(None, ("section", "rep"), "tp")
    whole = P(None, ("section", "rep"), None)
    return jax.shard_map(
        on_device,
        mesh=mesh,
        in_specs=(
            rows,
            rows,
            rows,
            rows,
            P(),
            P(),
            rows,
            rows,
            P("tp", None),
            P(),
            whole,
            slots,
            slots,
            slots,
            slots,
            slots,
            slots,
            slots,
        ),
        out_specs=(rows, whole, slots),
        check_vma=False,
    )
```

```python
import functools
import math

import jax
import jax.numpy as jnp
from jax import lax
from jax.experimental import pallas as pl
from jax.experimental.pallas import tpu as pltpu
from jax.sharding import PartitionSpec as P

MESH = pl.DeviceIdType.MESH
F32 = jnp.float32
BF16 = jnp.bfloat16
LOG2E = 1.0 / math.log(2.0)
LANES = 128
TILE = 16
PARTS = 2


def iota(shape, axis):
    return lax.broadcasted_iota(jnp.int32, shape, axis)


def dot(a, b):
    return jnp.dot(a, b, preferred_element_type=F32)


def dot_nt(a, b, precision=None):
    return lax.dot_general(
        a, b, (((1,), (1,)), ((), ())), preferred_element_type=F32, precision=precision
    )


def one_hot(mask):
    return jnp.where(mask, 1.0, 0.0).astype(BF16)


def split_two(x):
    high = x.astype(BF16)
    return high, (x - high.astype(F32)).astype(BF16)


def body(
    dims,
    pq_hbm,
    pk_hbm,
    pv_hbm,
    gate_hbm,
    len_hbm,
    dg_hbm,
    dgv_hbm,
    ck_hbm,
    cv_hbm,
    w_hbm,
    gain_hbm,
    si_hbm,
    sq_hbm,
    sk_hbm,
    sv_hbm,
    sg_hbm,
    fq_hbm,
    fk_hbm,
    fv_hbm,
    po,
    do,
    so,
    pq,
    pk,
    pv,
    gate,
    len_s,
    dg_s,
    dgv,
    ck,
    cv,
    w,
    gain,
    si,
    sq,
    sk,
    sv,
    sg,
    fq,
    fk,
    fv,
    rowf,
    colm,
    colw,
    state,
    own,
    gamma,
    sel_lin,
    sel_soft,
    send_q,
    recv_q,
    res_q,
    send_r,
    recv_r,
    send_s,
    recv_a,
    send_b,
    recv_b,
    send_t,
    recv_t,
    part_f,
    part_b,
    recv_p,
    base_of,
    gain_of,
    rows_of,
    in_sem,
    q_sem,
    r_sem,
    a_sem,
    b_sem,
    t_sem,
    rs_send,
    rs_recv,
    ag_send,
    ag_recv,
    pass_send,
):
    sections, reps, tps, held, length, heads, steps, q_heads, model = dims
    groups = sections * reps
    total = groups * held
    me_s = lax.axis_index("section")
    me_r = lax.axis_index("rep")
    me_p = lax.axis_index("tp")
    me_g = me_s * reps + me_r
    first = me_g * held
    per_owner = steps * 2 // tps
    me_y = me_p // 2
    me_c = me_p % 2
    lin_rows = heads * steps
    soft_rows = q_heads * steps

    owners = tps // 2
    sibling = (me_s, me_r, me_p + 1 - 2 * me_c)

    deep = 2 * sections
    across = reps // 2
    me_z = (me_r // across) * sections + me_s
    me_x = lax.rem(me_r, across)

    def ring(me, size):
        return {d: lax.rem(me + d, size) for d in range(size)}

    def hops(d, size):
        return min(d, size - d)

    z_at = ring(me_z, deep)
    x_at = ring(me_x, across)
    section_at = {d: lax.rem(z, sections) for d, z in z_at.items()}
    rep_at = {d: lax.div(z, sections) * across for d, z in z_at.items()}
    far_first = sorted(
        ((dz, dx) for dz in range(deep) for dx in range(across) if dz or dx),
        key=lambda d: -hops(d[0], deep) - hops(d[1], across),
    )
    y_at = ring(me_y, owners)

    def along_y(off):
        return y_at[off]

    barrier = pltpu.get_barrier_semaphore()

    for dz, dx in far_first:
        pl.semaphore_signal(
            barrier,
            inc=1,
            device_id=(section_at[dz], rep_at[dz] + x_at[dx], me_p),
            device_id_type=MESH,
        )
    for off in range(1, tps):
        pl.semaphore_signal(
            barrier,
            inc=1,
            device_id=(me_s, me_r, lax.rem(me_p + off, tps)),
            device_id_type=MESH,
        )

    y0 = me_y * per_owner
    loads = {}
    for place, (name, src, dst) in enumerate(
        (
            ("dgv", dgv_hbm, dgv),
            ("sq", sq_hbm, sq),
            ("dg", dg_hbm, dg_s),
            ("len", len_hbm, len_s),
            ("gate", gate_hbm, gate),
            ("pk", pk_hbm, pk),
            ("pv", pv_hbm, pv),
            ("pq", pq_hbm, pq),
            ("fq", fq_hbm, fq),
            ("fk", fk_hbm, fk),
            ("fv", fv_hbm, fv),
            ("sk", sk_hbm, sk),
            ("sv", sv_hbm, sv),
            ("sg", sg_hbm, sg),
            ("w", w_hbm, w),
            ("ck", ck_hbm, ck),
            ("cv", cv_hbm, cv),
            ("si", si_hbm.at[pl.ds(y0, per_owner)], si),
            ("gain", gain_hbm, gain),
        )
    ):
        loads[name] = pltpu.make_async_copy(src, dst, in_sem.at[place])
        loads[name].start()

    loads["dgv"].wait()
    mine = dgv[...] == me_g
    mine_rows = jnp.broadcast_to(one_hot(mine), (16, total))
    before = one_hot(iota((total, total), 0) < iota((total, total), 1))
    rank = dot(mine_rows, before)[0:1]
    slot_row = lax.rem(iota((soft_rows * held, total), 0), held).astype(F32)
    slot_of = one_hot(jnp.where(mine, rank, -1.0) == slot_row)
    slot_lin = slot_of[: lin_rows * held]

    def rep_rows(rows_each):
        shape = (rows_each * reps, total)
        source_rep = lax.rem(iota(shape, 1) // held, reps)
        return one_hot(iota(shape, 0) // rows_each == source_rep)

    def spread(rows_each, slots):
        picked = dot_nt(rep_rows(rows_each), slots)
        same = lax.rem(iota(picked.shape, 0), rows_each) == iota(picked.shape, 1) // held
        return jnp.where(same, picked, 0.0).astype(BF16)

    def by_row(ref, count):
        pieces = [
            ref[i, :, a * LANES : (a + 1) * LANES].astype(F32)
            for a in range(count)
            for i in range(steps)
        ]
        return jnp.concatenate(pieces, axis=0).astype(BF16)

    loads["sq"].wait()
    spread_lin = spread(lin_rows, slot_lin)
    blocks = dot(spread_lin, by_row(sq, heads)).astype(BF16)
    send_q[...] = blocks.reshape(reps, lin_rows, LANES)

    for name in ("fq", "fk", "fv"):
        loads[name].wait()
    soft_blocks = dot(spread(soft_rows, slot_of), by_row(fq, q_heads)).astype(BF16)
    send_s[:, :soft_rows, :] = soft_blocks.reshape(reps, soft_rows, LANES)
    fresh = jnp.concatenate([by_row(fk, 1).astype(F32), by_row(fv, 1).astype(F32)], axis=0)
    fresh_spread = spread_lin[:, : 2 * steps * held]
    fresh_blocks = dot(fresh_spread, fresh.astype(BF16)).astype(BF16)
    send_s[:, soft_rows:, :] = fresh_blocks.reshape(reps, lin_rows, LANES)

    pl.semaphore_wait(barrier, groups - 1 + tps - 1)

    def to_groups(src, dst, sems):
        for dz, dx in far_first:
            peer_r = rep_at[dz] + x_at[dx]
            pltpu.make_async_remote_copy(
                src_ref=src.at[peer_r],
                dst_ref=dst.at[me_g],
                send_sem=sems.at[0],
                recv_sem=sems.at[1],
                device_id=(section_at[dz], peer_r, me_p),
                device_id_type=MESH,
            ).start()
        dst[me_g] = src[me_r]

    def all_bytes(dst, sem):
        view = dst.at[pl.ds(0, dst.shape[0] - 1)]
        pltpu.make_async_copy(view, view, sem).wait()

    def rep_copy(off):
        peer_r = lax.rem(me_r + off, reps)
        return pltpu.make_async_remote_copy(
            src_ref=send_s.at[peer_r],
            dst_ref=recv_a.at[me_r],
            send_sem=a_sem.at[0],
            recv_sem=a_sem.at[1],
            device_id=(me_s, peer_r, me_p),
            device_id_type=MESH,
        )

    def section_copy(off):
        peer_s = lax.rem(me_s + off, sections)
        return pltpu.make_async_remote_copy(
            src_ref=send_b.at[peer_s],
            dst_ref=recv_b.at[me_s],
            send_sem=b_sem.at[0],
            recv_sem=b_sem.at[1],
            device_id=(peer_s, me_r, me_p),
            device_id_type=MESH,
        )

    to_groups(send_q, recv_q, q_sem)
    for off in range(1, reps):
        rep_copy(off).start()
    recv_a[me_r] = send_s[me_r]

    loads["dg"].wait()
    loads["len"].wait()
    loads["gate"].wait()
    count = held * heads
    shape = (count, length)
    own_len = [len_s[first + k] for k in range(held)]
    logs = jnp.log(jnp.concatenate([gate[k] for k in range(held)], axis=0))
    len_rows = jnp.zeros(shape, jnp.int32)
    for k in range(held):
        len_rows = jnp.where(iota(shape, 0) // heads == k, own_len[k], len_rows)
    inside = iota(shape, 1) < len_rows
    logs = jnp.where(inside, logs, 0.0)
    p1, rest = split_two(logs)
    rest = logs - p1.astype(F32)
    p2, p3 = split_two(rest)
    upto = one_hot(iota((length, length), 0) <= iota((length, length), 1))
    upto_t = one_hot(iota((length, length), 1) <= iota((length, length), 0))
    cum_rows = (dot(p1, upto) + dot(p2, upto) + dot(p3, upto)) * LOG2E
    cum_cols = (dot_nt(upto_t, p1) + dot_nt(upto_t, p2) + dot_nt(upto_t, p3)) * LOG2E
    shape = (length, count)
    len_cols = jnp.zeros(shape, jnp.int32)
    for k in range(held):
        len_cols = jnp.where(iota(shape, 1) // heads == k, own_len[k], len_cols)
    inside_cols = iota(shape, 0) < len_cols
    decays = jnp.where(inside_cols, jnp.exp2(cum_cols[length - 1 :] - cum_cols), 0.0)
    cum_cols = jnp.where(inside_cols, cum_cols, -jnp.inf)
    for k in range(held):
        rows = slice(k * heads, (k + 1) * heads)
        rowf[k] = cum_rows[rows]
        colm[k] = cum_cols[:, rows]
        colw[k] = decays[:, rows]

    loads["pk"].wait()
    loads["pv"].wait()

    def remember(k, carry):
        for h in range(heads):
            lanes = slice(h * LANES, (h + 1) * LANES)
            high, low = split_two(pv[k, :, lanes].astype(F32) * colw[k, :, h : h + 1])
            both = lax.dot_general(
                pk[k, :, lanes],
                jnp.concatenate([high, low], axis=1),
                (((0,), (0,)), ((), ())),
                preferred_element_type=F32,
            )
            high, low = split_two(both[:, :LANES] + both[:, LANES:])
            state[k, h, :LANES, :] = high
            state[k, h, LANES:, :] = low
        return carry

    lax.fori_loop(0, held, remember, 0)

    loads["pq"].wait()
    mid = length // 2

    def prompt(k, carry):
        causal = iota((mid, mid), 0) >= iota((mid, mid), 1)
        for h in range(heads):
            lanes = slice(h * LANES, (h + 1) * LANES)
            scores = dot_nt(pq[k, :, lanes], pk[k, :, lanes])
            row = rowf[k, h : h + 1, :]
            col = colm[k, :, h : h + 1]
            values = pv[k, :, lanes]
            gap = jnp.where(causal, col[:mid] - row[:, :mid], -jnp.inf)
            top = (jnp.exp2(gap) * scores[:mid, :mid]).astype(BF16)
            low_left = (jnp.exp2(col[mid:] - row[:, :mid]) * scores[mid:, :mid]).astype(BF16)
            gap = jnp.where(causal, col[mid:] - row[:, mid:], -jnp.inf)
            low_right = (jnp.exp2(gap) * scores[mid:, mid:]).astype(BF16)
            low = jnp.concatenate([low_left, low_right], axis=1)
            po[k, :mid, lanes] = dot(top, values[:mid]).astype(BF16)
            po[k, mid:, lanes] = dot(low, values).astype(BF16)
        return carry

    for name in ("sk", "sv", "sg"):
        loads[name].wait()
    eye = jnp.where(iota((held, held), 0) == iota((held, held), 1), 1.0, 0.0)
    gates = [dot_nt(eye, sg[i], lax.Precision.HIGHEST) for i in range(steps)]
    for h in range(heads):
        lanes = slice(h * LANES, (h + 1) * LANES)
        running = jnp.ones((held, 1), F32)
        for i in range(steps):
            running = running * gates[i][:, h : h + 1]
            gamma[i, :, lanes] = jnp.broadcast_to(running, (held, LANES))
            query = sq[i, :, lanes].astype(F32)
            added = jnp.zeros((held, LANES), F32)
            since = jnp.ones((held, 1), F32)
            for u in range(i, -1, -1):
                pair = jnp.sum(query * sk[u, :, lanes].astype(F32), axis=1, keepdims=True)
                added = added + (since * pair) * sv[u, :, lanes].astype(F32)
                since = since * gates[u][:, h : h + 1]
            own[i, :, lanes] = added

    def pick(rows_each, slots):
        shape = (total, rows_each * groups)
        source = one_hot(iota(shape, 0) // held == iota(shape, 1) // rows_each)
        picked = dot(slots, source)
        same = iota(picked.shape, 0) // held == lax.rem(iota(picked.shape, 1), rows_each)
        return jnp.where(same, picked, 0.0).astype(BF16)

    sel_lin[...] = pick(lin_rows, slot_lin)
    target_rep = [lax.rem(dg_s[first + k], reps) for k in range(held)]
    bound_for = []
    for r in range(reps):
        found = jnp.int32(0)
        for k in range(held):
            found = jnp.where(target_rep[k] == r, k, found)
        bound_for.append(found)
    each = held // sections
    onward = []
    for s in range(sections):
        chosen = [jnp.int32(0)] * each
        seen = jnp.int32(0)
        for k in range(held):
            group = dg_s[(s * reps + me_r) * held + k]
            hit = lax.div(group, reps) == me_s
            for c in range(each):
                chosen[c] = jnp.where(hit & (seen == c), lax.rem(group, reps), chosen[c])
            seen = seen + jnp.where(hit, 1, 0)
        onward.append(chosen)
    all_bytes(recv_q, q_sem.at[1])
    head_of_row = iota((lin_rows, LANES), 0) // steps
    for k in range(held):
        asked = recv_q[dg_s[first + k]].astype(F32)
        apart = []
        for h in range(heads):
            apart += [jnp.where(head_of_row == h, asked, 0.0).astype(BF16)] * 2
        states = state[k].reshape(2 * heads * LANES, LANES)
        res_q[k] = dot(jnp.concatenate(apart, axis=1), states).astype(BF16)
    for r in range(reps):
        send_r[r] = res_q[bound_for[r]]
    to_groups(send_r, recv_r, r_sem)

    all_bytes(recv_a, a_sem.at[1])
    for s in range(sections):
        for c in range(each):
            send_b[s, c] = recv_a[onward[s][c]]
    for off in range(1, sections):
        section_copy(off).start()
    recv_b[me_s] = send_b[me_s]

    sel_soft[...] = pick(soft_rows, slot_of)
    early = held // 2
    lax.fori_loop(0, early, prompt, 0)

    mine_each = held // 2
    owned = per_owner * mine_each
    blocks_of = TILE // owned
    wide = model // blocks_of
    narrow = wide // PARTS
    loads["si"].wait()
    loads["gain"].wait()
    block_row = iota((TILE, wide), 0) // owned
    shape = (TILE, per_owner * held)
    row = lax.rem(iota(shape, 0), owned)
    wanted = (row // mine_each) * held + me_c * mine_each + lax.rem(row, mine_each)
    own_rows = one_hot(wanted == iota(shape, 1))
    inputs = jnp.concatenate([si[n].astype(F32) for n in range(per_owner)], axis=0).astype(BF16)
    base = jnp.zeros((TILE, wide), F32)
    gains = jnp.zeros((TILE, wide), F32)
    for b in range(blocks_of):
        cols = slice(b * wide, (b + 1) * wide)
        base = jnp.where(block_row == b, dot(own_rows, inputs[:, cols]), base)
        gains = jnp.where(block_row == b, gain[:, cols], gains)
    base_of[...] = base
    gain_of[...] = gains

    loads["w"].wait()
    all_bytes(recv_r, r_sem.at[1])
    carried = dot(sel_lin[...], recv_r[...].reshape(groups * lin_rows, LANES))
    hidden = []
    for i in range(steps):
        over_heads = []
        for h in range(heads):
            lanes = slice(h * LANES, (h + 1) * LANES)
            rows = slice((h * steps + i) * held, (h * steps + i + 1) * held)
            over_heads.append(gamma[i, :, lanes] * carried[rows] + own[i, :, lanes])
        hidden.append(jnp.concatenate(over_heads, axis=1))
    hidden = jnp.concatenate(hidden, axis=0).astype(BF16)
    by_distance = sorted(range(1, owners), key=lambda o: -min(o, owners - o))
    peers = [along_y(off) * 2 + core for off in by_distance for core in range(2)]
    peers.append(me_p + 1 - 2 * me_c)

    def sum_copy(part, peer):
        return pltpu.make_async_remote_copy(
            src_ref=part_b.at[part, peer],
            dst_ref=recv_p.at[part, me_p],
            send_sem=rs_send.at[part, peer],
            recv_sem=rs_recv.at[part, me_p],
            device_id=(me_s, me_r, peer),
            device_id_type=MESH,
        )

    for part in range(PARTS):
        for b in range(blocks_of):
            start = b * wide + part * narrow
            partial = dot(hidden, w[:, start : start + narrow])
            for i in range(steps):
                for core in range(2):
                    row = b * owned + (i % per_owner) * mine_each
                    here = i * held + core * mine_each
                    part_f[part, i // per_owner * 2 + core, row : row + mine_each, :] = partial[
                        here : here + mine_each
                    ]
        part_b[part] = part_f[part].astype(BF16)
        for peer in peers:
            sum_copy(part, peer).start()

    loads["ck"].wait()
    loads["cv"].wait()
    all_bytes(recv_b, b_sem.at[1])
    scale = LOG2E / math.sqrt(LANES)

    def soft(k):
        section = lax.div(dg_s[first + k], reps)
        place_of = jnp.int32(0)
        for k2 in range(held):
            same = (lax.div(dg_s[first + k2], reps) == section) & (k2 < k)
            place_of = place_of + jnp.where(same, 1, 0)
        block = recv_b[section, jnp.minimum(place_of, each - 1)]
        asked = block[:soft_rows]
        fresh_rows = block[soft_rows:]
        scores = dot_nt(asked, ck[k]) * scale
        scores = jnp.where(iota(scores.shape, 1) < len_s[first + k], scores, -jnp.inf)
        news = dot_nt(asked, fresh_rows) * scale
        lane = iota(news.shape, 1)
        seen = (lane < steps) & (lane <= lax.rem(iota(news.shape, 0), steps))
        news = jnp.where(seen, news, -jnp.inf)
        peak = jnp.maximum(
            jnp.max(scores, axis=1, keepdims=True), jnp.max(news, axis=1, keepdims=True)
        )
        scores = jnp.exp2(scores - peak)
        news = jnp.exp2(news - peak)
        bottom = jnp.sum(scores, axis=1, keepdims=True) + jnp.sum(news, axis=1, keepdims=True)
        probs = (scores / bottom).astype(BF16)
        fresh_probs = (news / bottom).astype(BF16).astype(F32)
        fresh_values = fresh_rows.astype(F32)
        mixed = dot(probs, cv[k])
        for u in range(steps):
            mixed = mixed + fresh_probs[:, u : u + 1] * fresh_values[steps + u : steps + u + 1]
        return mixed.astype(BF16)

    def requests_for(r):
        found = jnp.int32(0)
        for k in range(held):
            found = jnp.where(target_rep[k] == r, k, found)
        return found

    def answer_copy(peer_s, peer_r):
        return pltpu.make_async_remote_copy(
            src_ref=send_t.at[peer_r],
            dst_ref=recv_t.at[me_g],
            send_sem=t_sem.at[0],
            recv_sem=t_sem.at[1],
            device_id=(peer_s, peer_r, me_p),
            device_id_type=MESH,
        )

    rep_steps = sorted(
        ((dz, dx) for dz in (0, sections) for dx in range(across)),
        key=lambda d: -hops(d[0], deep) - hops(d[1], across),
    )
    batch = max(held // 2, 1)
    for start in range(0, held, batch):
        chosen = rep_steps[start : start + batch]
        targets = [rep_at[dz] + x_at[dx] for dz, dx in chosen]
        answers = [soft(requests_for(r)) for r in targets]
        for r, answer in zip(targets, answers):
            send_t[r] = answer
        for (dz, dx), r, answer in zip(chosen, targets, answers):
            for ds in range(sections):
                if dz or dx or ds:
                    answer_copy(lax.rem(me_s + ds, sections), r).start()
                else:
                    recv_t[me_g] = answer

    summed = []
    for part in range(PARTS):
        here = slice(part * narrow, (part + 1) * narrow)
        value = part_f[part, me_p] + base_of[:, here]
        for source in reversed(peers):
            block = recv_p.at[part, source]
            pltpu.make_async_copy(block, block, rs_recv.at[part, source]).wait()
            value = value + recv_p[part, source].astype(F32)
        summed.append(value)
    square = jnp.sum(sum(value * value for value in summed), axis=1, keepdims=True)
    square = jnp.broadcast_to(square, (TILE, LANES))
    shift = TILE // 2
    while shift >= owned:
        square = square + pltpu.roll(square, shift, 0)
        shift //= 2
    spread_of = jnp.sqrt(square[:, :1] / model + 1e-06)

    def gather_copy(off):
        peer = along_y(off) * 2 + me_c
        return pltpu.make_async_remote_copy(
            src_ref=rows_of.at[me_p],
            dst_ref=rows_of.at[me_p],
            send_sem=ag_send.at[peer],
            recv_sem=ag_recv.at[me_p],
            device_id=(me_s, me_r, peer),
            device_id_type=MESH,
        )

    def pass_copy(y):
        source = y * 2 + me_c
        return pltpu.make_async_remote_copy(
            src_ref=rows_of.at[source],
            dst_ref=rows_of.at[source],
            send_sem=pass_send.at[y],
            recv_sem=ag_recv.at[source],
            device_id=sibling,
            device_id_type=MESH,
        )

    def landed(source):
        block = rows_of.at[source]
        pltpu.make_async_copy(block, block, ag_recv.at[source]).wait()

    for part in range(PARTS):
        here = slice(part * narrow, (part + 1) * narrow)
        rows_of[me_p, part] = (summed[part] / spread_of * gain_of[:, here]).astype(BF16)
    for off in by_distance:
        gather_copy(off).start()
    pass_copy(me_y).start()

    lax.fori_loop(early, held, prompt, 0)

    for off in reversed(by_distance):
        landed(along_y(off) * 2 + me_c)
        pass_copy(along_y(off)).start()

    all_bytes(recv_t, t_sem.at[1])
    placed = dot(sel_soft[...], recv_t[...].reshape(groups * soft_rows, LANES))
    for a in range(q_heads):
        for i in range(steps):
            rows = slice((a * steps + i) * held, (a * steps + i + 1) * held)
            so[i, :, a * LANES : (a + 1) * LANES] = placed[rows].astype(BF16)

    all_bytes(recv_q, q_sem.at[0])
    all_bytes(recv_r, r_sem.at[0])
    all_bytes(recv_a, a_sem.at[0])
    all_bytes(recv_b, b_sem.at[0])
    all_bytes(recv_t, t_sem.at[0])
    for part in range(PARTS):
        for peer in peers:
            sum_copy(part, peer).wait_send()

    shape = (blocks_of * per_owner * held, 2 * TILE)
    slot = lax.rem(iota(shape, 0), held)
    step = lax.rem(iota(shape, 0) // held, per_owner)
    block = iota(shape, 0) // (held * per_owner)
    wanted = (slot // mine_each) * TILE + block * owned + step * mine_each
    unpack = one_hot(wanted + lax.rem(slot, mine_each) == iota(shape, 1))
    for off in [0] + list(reversed(by_distance)):
        y = along_y(off)
        landed(y * 2 + 1 - me_c)
        for part in range(PARTS):
            pair = rows_of[pl.ds(y * 2, 2), part].reshape(2 * TILE, narrow)
            ordered = dot(unpack, pair)
            for b in range(blocks_of):
                start = b * wide + part * narrow
                for n in range(per_owner):
                    rows = slice((b * per_owner + n) * held, (b * per_owner + n + 1) * held)
                    do[y * per_owner + n, :, start : start + narrow] = ordered[rows].astype(BF16)
    for off in by_distance:
        gather_copy(off).wait_send()
    for y in range(owners):
        pass_copy(along_y(y)).wait_send()


def write_out(po, do, so, po_hbm, do_hbm, so_hbm, sem):
    held = po.shape[0]
    copies = [pltpu.make_async_copy(po.at[k], po_hbm.at[k], sem.at[k]) for k in range(held)]
    copies.append(pltpu.make_async_copy(do, do_hbm, sem.at[held]))
    copies.append(pltpu.make_async_copy(so, so_hbm, sem.at[held + 1]))
    for copy in copies:
        copy.start()
    for copy in copies:
        copy.wait()


def on_device(
    prefill_query,
    prefill_key,
    prefill_value,
    prefill_gate,
    lengths,
    decode_group,
    cache_keys,
    cache_values,
    out_weight,
    norm_gain,
    step_input,
    step_query,
    step_key,
    step_value,
    step_gate,
    soft_query,
    soft_new_key,
    soft_new_value,
):
    sections, reps, tps = (lax.axis_size(name) for name in ("section", "rep", "tp"))
    held, length, heads = prefill_gate.shape
    steps = step_query.shape[0]
    q_heads = soft_query.shape[2] // LANES
    model = out_weight.shape[1]
    groups = sections * reps
    width = heads * LANES
    per_owner = steps * 2 // tps
    narrow = model * per_owner * (held // 2) // TILE // PARTS
    lin_rows = heads * steps
    soft_rows = q_heads * steps
    total = groups * held
    dims = (sections, reps, tps, held, length, heads, steps, q_heads, model)
    operands = (
        prefill_query,
        prefill_key,
        prefill_value,
        jnp.transpose(prefill_gate, (0, 2, 1)),
        lengths,
        decode_group,
        decode_group.reshape(1, total),
        cache_keys,
        cache_values,
        out_weight,
        norm_gain.reshape(1, model),
        step_input,
        step_query,
        step_key,
        step_value,
        jnp.transpose(step_gate, (0, 2, 1)),
        soft_query,
        soft_new_key,
        soft_new_value,
    )
    vmem = pltpu.VMEM
    dma = pltpu.SemaphoreType.DMA
    scratch = [
        vmem((held, length, width), BF16),
        vmem((held, length, width), BF16),
        vmem((held, length, width), BF16),
        vmem((held, heads, length), F32),
        pltpu.SMEM((total,), jnp.int32),
        pltpu.SMEM((total,), jnp.int32),
        vmem((1, total), jnp.int32),
        vmem((held, length, LANES), BF16),
        vmem((held, length, LANES), BF16),
        vmem((width, model), BF16),
        vmem((1, model), F32),
        vmem((per_owner, held, model), BF16),
        vmem((steps, held, width), BF16),
        vmem((steps, held, width), BF16),
        vmem((steps, held, width), BF16),
        vmem((steps, heads, held), F32),
        vmem((steps, held, q_heads * LANES), BF16),
        vmem((steps, held, LANES), BF16),
        vmem((steps, held, LANES), BF16),
        vmem((held, heads, length), F32),
        vmem((held, length, heads), F32),
        vmem((held, length, heads), F32),
        vmem((held, heads, 2 * LANES, LANES), BF16),
        vmem((steps, held, width), F32),
        vmem((steps, held, width), F32),
        vmem((lin_rows * held, lin_rows * groups), BF16),
        vmem((soft_rows * held, soft_rows * groups), BF16),
        vmem((reps, lin_rows, LANES), BF16),
        vmem((groups, lin_rows, LANES), BF16),
        vmem((held, lin_rows, LANES), BF16),
        vmem((reps, lin_rows, LANES), BF16),
        vmem((groups, lin_rows, LANES), BF16),
        vmem((reps, soft_rows + lin_rows, LANES), BF16),
        vmem((reps, soft_rows + lin_rows, LANES), BF16),
        vmem((sections, held // sections, soft_rows + lin_rows, LANES), BF16),
        vmem((sections, held // sections, soft_rows + lin_rows, LANES), BF16),
        vmem((reps, soft_rows, LANES), BF16),
        vmem((groups, soft_rows, LANES), BF16),
        vmem((PARTS, tps, TILE, narrow), F32),
        vmem((PARTS, tps, TILE, narrow), BF16),
        vmem((PARTS, tps, TILE, narrow), BF16),
        vmem((TILE, PARTS * narrow), F32),
        vmem((TILE, PARTS * narrow), F32),
        vmem((tps, PARTS, TILE, narrow), BF16),
        dma((19,)),
        dma((2,)),
        dma((2,)),
        dma((2,)),
        dma((2,)),
        dma((2,)),
        dma((PARTS, tps)),
        dma((PARTS, tps)),
        dma((tps,)),
        dma((tps,)),
        dma((tps // 2,)),
    ]
    anywhere = pl.BlockSpec(memory_space=pl.ANY)
    results = pl.pallas_call(
        functools.partial(body, dims),
        out_shape=(
            vmem((held, length, width), BF16),
            vmem((steps, held, model), BF16),
            vmem((steps, held, q_heads * LANES), BF16),
        ),
        in_specs=[anywhere] * len(operands),
        out_specs=(pl.BlockSpec(memory_space=vmem),) * 3,
        scratch_shapes=scratch,
        compiler_params=pltpu.CompilerParams(
            collective_id=0, has_side_effects=True, vmem_limit_bytes=56 * 1024 * 1024
        ),
    )(*operands)
    results = [pltpu.with_memory_space_constraint(x, pltpu.VMEM) for x in results]
    return pl.pallas_call(
        write_out,
        out_shape=[jax.ShapeDtypeStruct(array.shape, array.dtype) for array in results],
        in_specs=[anywhere] * 3,
        out_specs=[anywhere] * 3,
        scratch_shapes=[dma((held + 2,))],
    )(*results)


def solution(mesh):
    rows = P(("section", "rep"), None, "tp")
    slots = P(None, ("section", "rep"), "tp")
    whole = P(None, ("section", "rep"), None)
    return jax.shard_map(
        on_device,
        mesh=mesh,
        in_specs=(
            rows,
            rows,
            rows,
            rows,
            P(),
            P(),
            rows,
            rows,
            P("tp", None),
            P(),
            whole,
            slots,
            slots,
            slots,
            slots,
            slots,
            slots,
            slots,
        ),
        out_specs=(rows, whole, slots),
        check_vma=False,
    )
```

```python
import functools
import math

import jax
import jax.numpy as jnp
from jax import lax
from jax.experimental import pallas as pl
from jax.experimental.pallas import tpu as pltpu
from jax.sharding import PartitionSpec as P

MESH = pl.DeviceIdType.MESH
F32 = jnp.float32
BF16 = jnp.bfloat16
LOG2E = 1.0 / math.log(2.0)
LANES = 128
TILE = 16
PARTS = 2


def iota(shape, axis):
    return lax.broadcasted_iota(jnp.int32, shape, axis)


def dot(a, b):
    return jnp.dot(a, b, preferred_element_type=F32)


def dot_nt(a, b, precision=None):
    return lax.dot_general(
        a, b, (((1,), (1,)), ((), ())), preferred_element_type=F32, precision=precision
    )


def one_hot(mask):
    return jnp.where(mask, 1.0, 0.0).astype(BF16)


def split_two(x):
    high = x.astype(BF16)
    return high, (x - high.astype(F32)).astype(BF16)


def body(
    dims,
    pq_hbm,
    pk_hbm,
    pv_hbm,
    gate_hbm,
    len_hbm,
    dg_hbm,
    dgv_hbm,
    ck_hbm,
    cv_hbm,
    w_hbm,
    gain_hbm,
    si_hbm,
    sq_hbm,
    sk_hbm,
    sv_hbm,
    sg_hbm,
    fq_hbm,
    fk_hbm,
    fv_hbm,
    po,
    do,
    so,
    pq,
    pk,
    pv,
    gate,
    len_s,
    dg_s,
    dgv,
    ck,
    cv,
    w,
    gain,
    si,
    sq,
    sk,
    sv,
    sg,
    fq,
    fk,
    fv,
    rowf,
    colm,
    colw,
    state,
    own,
    gamma,
    sel_lin,
    sel_soft,
    send_q,
    recv_q,
    res_q,
    send_r,
    recv_r,
    send_s,
    recv_a,
    send_b,
    recv_b,
    send_t,
    recv_t,
    part_f,
    part_b,
    recv_p,
    base_of,
    gain_of,
    rows_of,
    in_sem,
    q_sem,
    r_sem,
    a_sem,
    b_sem,
    t_sem,
    rs_send,
    rs_recv,
    ag_send,
    ag_recv,
    pass_send,
):
    sections, reps, tps, held, length, heads, steps, q_heads, model = dims
    groups = sections * reps
    total = groups * held
    me_s = lax.axis_index("section")
    me_r = lax.axis_index("rep")
    me_p = lax.axis_index("tp")
    me_g = me_s * reps + me_r
    first = me_g * held
    per_owner = steps * 2 // tps
    me_y = me_p // 2
    me_c = me_p % 2
    lin_rows = heads * steps
    soft_rows = q_heads * steps

    owners = tps // 2
    sibling = (me_s, me_r, me_p + 1 - 2 * me_c)

    deep = 2 * sections
    across = reps // 2
    me_z = (me_r // across) * sections + me_s
    me_x = lax.rem(me_r, across)

    def ring(me, size):
        return {d: lax.rem(me + d, size) for d in range(size)}

    def hops(d, size):
        return min(d, size - d)

    z_at = ring(me_z, deep)
    x_at = ring(me_x, across)
    section_at = {d: lax.rem(z, sections) for d, z in z_at.items()}
    rep_at = {d: lax.div(z, sections) * across for d, z in z_at.items()}
    far_first = sorted(
        ((dz, dx) for dz in range(deep) for dx in range(across) if dz or dx),
        key=lambda d: -hops(d[0], deep) - hops(d[1], across),
    )
    y_at = ring(me_y, owners)

    def along_y(off):
        return y_at[off]

    barrier = pltpu.get_barrier_semaphore()

    for dz, dx in far_first:
        pl.semaphore_signal(
            barrier,
            inc=1,
            device_id=(section_at[dz], rep_at[dz] + x_at[dx], me_p),
            device_id_type=MESH,
        )
    for off in range(1, tps):
        pl.semaphore_signal(
            barrier,
            inc=1,
            device_id=(me_s, me_r, lax.rem(me_p + off, tps)),
            device_id_type=MESH,
        )

    y0 = me_y * per_owner
    loads = {}
    for place, (name, src, dst) in enumerate(
        (
            ("dgv", dgv_hbm, dgv),
            ("sq", sq_hbm, sq),
            ("dg", dg_hbm, dg_s),
            ("len", len_hbm, len_s),
            ("gate", gate_hbm, gate),
            ("pk", pk_hbm, pk),
            ("pv", pv_hbm, pv),
            ("pq", pq_hbm, pq),
            ("fq", fq_hbm, fq),
            ("fk", fk_hbm, fk),
            ("fv", fv_hbm, fv),
            ("sk", sk_hbm, sk),
            ("sv", sv_hbm, sv),
            ("sg", sg_hbm, sg),
            ("w", w_hbm, w),
            ("ck", ck_hbm, ck),
            ("cv", cv_hbm, cv),
            ("si", si_hbm.at[pl.ds(y0, per_owner)], si),
            ("gain", gain_hbm, gain),
        )
    ):
        loads[name] = pltpu.make_async_copy(src, dst, in_sem.at[place])
        loads[name].start()

    loads["dgv"].wait()
    mine = dgv[...] == me_g
    mine_rows = jnp.broadcast_to(one_hot(mine), (16, total))
    before = one_hot(iota((total, total), 0) < iota((total, total), 1))
    rank = dot(mine_rows, before)[0:1]
    slot_row = lax.rem(iota((soft_rows * held, total), 0), held).astype(F32)
    slot_of = one_hot(jnp.where(mine, rank, -1.0) == slot_row)
    slot_lin = slot_of[: lin_rows * held]

    def rep_rows(rows_each):
        shape = (rows_each * reps, total)
        source_rep = lax.rem(iota(shape, 1) // held, reps)
        return one_hot(iota(shape, 0) // rows_each == source_rep)

    def spread(rows_each, slots):
        picked = dot_nt(rep_rows(rows_each), slots)
        same = lax.rem(iota(picked.shape, 0), rows_each) == iota(picked.shape, 1) // held
        return jnp.where(same, picked, 0.0).astype(BF16)

    def by_row(ref, count):
        pieces = [
            ref[i, :, a * LANES : (a + 1) * LANES].astype(F32)
            for a in range(count)
            for i in range(steps)
        ]
        return jnp.concatenate(pieces, axis=0).astype(BF16)

    loads["sq"].wait()
    spread_lin = spread(lin_rows, slot_lin)
    blocks = dot(spread_lin, by_row(sq, heads)).astype(BF16)
    send_q[...] = blocks.reshape(reps, lin_rows, LANES)

    for name in ("fq", "fk", "fv"):
        loads[name].wait()
    soft_blocks = dot(spread(soft_rows, slot_of), by_row(fq, q_heads)).astype(BF16)
    send_s[:, :soft_rows, :] = soft_blocks.reshape(reps, soft_rows, LANES)
    fresh = jnp.concatenate([by_row(fk, 1).astype(F32), by_row(fv, 1).astype(F32)], axis=0)
    fresh_spread = spread_lin[:, : 2 * steps * held]
    fresh_blocks = dot(fresh_spread, fresh.astype(BF16)).astype(BF16)
    send_s[:, soft_rows:, :] = fresh_blocks.reshape(reps, lin_rows, LANES)

    pl.semaphore_wait(barrier, groups - 1 + tps - 1)

    def to_groups(src, dst, sems):
        for dz, dx in far_first:
            peer_r = rep_at[dz] + x_at[dx]
            pltpu.make_async_remote_copy(
                src_ref=src.at[peer_r],
                dst_ref=dst.at[me_g],
                send_sem=sems.at[0],
                recv_sem=sems.at[1],
                device_id=(section_at[dz], peer_r, me_p),
                device_id_type=MESH,
            ).start()
        dst[me_g] = src[me_r]

    def all_bytes(dst, sem):
        view = dst.at[pl.ds(0, dst.shape[0] - 1)]
        pltpu.make_async_copy(view, view, sem).wait()

    def rep_copy(off):
        peer_r = lax.rem(me_r + off, reps)
        return pltpu.make_async_remote_copy(
            src_ref=send_s.at[peer_r],
            dst_ref=recv_a.at[me_r],
            send_sem=a_sem.at[0],
            recv_sem=a_sem.at[1],
            device_id=(me_s, peer_r, me_p),
            device_id_type=MESH,
        )

    def section_copy(off):
        peer_s = lax.rem(me_s + off, sections)
        return pltpu.make_async_remote_copy(
            src_ref=send_b.at[peer_s],
            dst_ref=recv_b.at[me_s],
            send_sem=b_sem.at[0],
            recv_sem=b_sem.at[1],
            device_id=(peer_s, me_r, me_p),
            device_id_type=MESH,
        )

    to_groups(send_q, recv_q, q_sem)
    for off in range(1, reps):
        rep_copy(off).start()
    recv_a[me_r] = send_s[me_r]

    loads["dg"].wait()
    loads["len"].wait()
    loads["gate"].wait()
    count = held * heads
    shape = (count, length)
    own_len = [len_s[first + k] for k in range(held)]
    logs = jnp.log(jnp.concatenate([gate[k] for k in range(held)], axis=0))
    len_rows = jnp.zeros(shape, jnp.int32)
    for k in range(held):
        len_rows = jnp.where(iota(shape, 0) // heads == k, own_len[k], len_rows)
    inside = iota(shape, 1) < len_rows
    logs = jnp.where(inside, logs, 0.0)
    p1, rest = split_two(logs)
    rest = logs - p1.astype(F32)
    p2, p3 = split_two(rest)
    upto = one_hot(iota((length, length), 0) <= iota((length, length), 1))
    upto_t = one_hot(iota((length, length), 1) <= iota((length, length), 0))
    cum_rows = (dot(p1, upto) + dot(p2, upto) + dot(p3, upto)) * LOG2E
    cum_cols = (dot_nt(upto_t, p1) + dot_nt(upto_t, p2) + dot_nt(upto_t, p3)) * LOG2E
    shape = (length, count)
    len_cols = jnp.zeros(shape, jnp.int32)
    for k in range(held):
        len_cols = jnp.where(iota(shape, 1) // heads == k, own_len[k], len_cols)
    inside_cols = iota(shape, 0) < len_cols
    decays = jnp.where(inside_cols, jnp.exp2(cum_cols[length - 1 :] - cum_cols), 0.0)
    cum_cols = jnp.where(inside_cols, cum_cols, -jnp.inf)
    for k in range(held):
        rows = slice(k * heads, (k + 1) * heads)
        rowf[k] = cum_rows[rows]
        colm[k] = cum_cols[:, rows]
        colw[k] = decays[:, rows]

    loads["pk"].wait()
    loads["pv"].wait()

    def remember(k, carry):
        for h in range(heads):
            lanes = slice(h * LANES, (h + 1) * LANES)
            high, low = split_two(pv[k, :, lanes].astype(F32) * colw[k, :, h : h + 1])
            both = lax.dot_general(
                pk[k, :, lanes],
                jnp.concatenate([high, low], axis=1),
                (((0,), (0,)), ((), ())),
                preferred_element_type=F32,
            )
            high, low = split_two(both[:, :LANES] + both[:, LANES:])
            state[k, h, :LANES, :] = high
            state[k, h, LANES:, :] = low
        return carry

    lax.fori_loop(0, held, remember, 0)

    loads["pq"].wait()
    mid = length // 2

    def prompt(k, carry):
        causal = iota((mid, mid), 0) >= iota((mid, mid), 1)
        for h in range(heads):
            lanes = slice(h * LANES, (h + 1) * LANES)
            scores = dot_nt(pq[k, :, lanes], pk[k, :, lanes])
            row = rowf[k, h : h + 1, :]
            col = colm[k, :, h : h + 1]
            values = pv[k, :, lanes]
            gap = jnp.where(causal, col[:mid] - row[:, :mid], -jnp.inf)
            top = (jnp.exp2(gap) * scores[:mid, :mid]).astype(BF16)
            low_left = (jnp.exp2(col[mid:] - row[:, :mid]) * scores[mid:, :mid]).astype(BF16)
            gap = jnp.where(causal, col[mid:] - row[:, mid:], -jnp.inf)
            low_right = (jnp.exp2(gap) * scores[mid:, mid:]).astype(BF16)
            low = jnp.concatenate([low_left, low_right], axis=1)
            po[k, :mid, lanes] = dot(top, values[:mid]).astype(BF16)
            po[k, mid:, lanes] = dot(low, values).astype(BF16)
        return carry

    for name in ("sk", "sv", "sg"):
        loads[name].wait()
    eye = jnp.where(iota((held, held), 0) == iota((held, held), 1), 1.0, 0.0)
    gates = [dot_nt(eye, sg[i], lax.Precision.HIGHEST) for i in range(steps)]
    for h in range(heads):
        lanes = slice(h * LANES, (h + 1) * LANES)
        running = jnp.ones((held, 1), F32)
        for i in range(steps):
            running = running * gates[i][:, h : h + 1]
            gamma[i, :, lanes] = jnp.broadcast_to(running, (held, LANES))
            query = sq[i, :, lanes].astype(F32)
            added = jnp.zeros((held, LANES), F32)
            since = jnp.ones((held, 1), F32)
            for u in range(i, -1, -1):
                pair = jnp.sum(query * sk[u, :, lanes].astype(F32), axis=1, keepdims=True)
                added = added + (since * pair) * sv[u, :, lanes].astype(F32)
                since = since * gates[u][:, h : h + 1]
            own[i, :, lanes] = added

    def pick(rows_each, slots):
        shape = (total, rows_each * groups)
        source = one_hot(iota(shape, 0) // held == iota(shape, 1) // rows_each)
        picked = dot(slots, source)
        same = iota(picked.shape, 0) // held == lax.rem(iota(picked.shape, 1), rows_each)
        return jnp.where(same, picked, 0.0).astype(BF16)

    sel_lin[...] = pick(lin_rows, slot_lin)
    target_rep = [lax.rem(dg_s[first + k], reps) for k in range(held)]
    bound_for = []
    for r in range(reps):
        found = jnp.int32(0)
        for k in range(held):
            found = jnp.where(target_rep[k] == r, k, found)
        bound_for.append(found)
    each = held // sections
    onward = []
    for s in range(sections):
        chosen = [jnp.int32(0)] * each
        seen = jnp.int32(0)
        for k in range(held):
            group = dg_s[(s * reps + me_r) * held + k]
            hit = lax.div(group, reps) == me_s
            for c in range(each):
                chosen[c] = jnp.where(hit & (seen == c), lax.rem(group, reps), chosen[c])
            seen = seen + jnp.where(hit, 1, 0)
        onward.append(chosen)
    all_bytes(recv_q, q_sem.at[1])
    head_of_row = iota((lin_rows, LANES), 0) // steps
    for k in range(held):
        asked = recv_q[dg_s[first + k]].astype(F32)
        apart = []
        for h in range(heads):
            apart += [jnp.where(head_of_row == h, asked, 0.0).astype(BF16)] * 2
        states = state[k].reshape(2 * heads * LANES, LANES)
        res_q[k] = dot(jnp.concatenate(apart, axis=1), states).astype(BF16)
    for r in range(reps):
        send_r[r] = res_q[bound_for[r]]
    to_groups(send_r, recv_r, r_sem)

    all_bytes(recv_a, a_sem.at[1])
    for s in range(sections):
        for c in range(each):
            send_b[s, c] = recv_a[onward[s][c]]
    for off in range(1, sections):
        section_copy(off).start()
    recv_b[me_s] = send_b[me_s]

    sel_soft[...] = pick(soft_rows, slot_of)
    early = held // 2 + held // 4
    lax.fori_loop(0, early, prompt, 0)

    mine_each = held // 2
    owned = per_owner * mine_each
    blocks_of = TILE // owned
    wide = model // blocks_of
    narrow = wide // PARTS
    loads["si"].wait()
    loads["gain"].wait()
    block_row = iota((TILE, wide), 0) // owned
    shape = (TILE, per_owner * held)
    row = lax.rem(iota(shape, 0), owned)
    wanted = (row // mine_each) * held + me_c * mine_each + lax.rem(row, mine_each)
    own_rows = one_hot(wanted == iota(shape, 1))
    inputs = jnp.concatenate([si[n].astype(F32) for n in range(per_owner)], axis=0).astype(BF16)
    base = jnp.zeros((TILE, wide), F32)
    gains = jnp.zeros((TILE, wide), F32)
    for b in range(blocks_of):
        cols = slice(b * wide, (b + 1) * wide)
        base = jnp.where(block_row == b, dot(own_rows, inputs[:, cols]), base)
        gains = jnp.where(block_row == b, gain[:, cols], gains)
    base_of[...] = base
    gain_of[...] = gains

    loads["w"].wait()
    all_bytes(recv_r, r_sem.at[1])
    carried = dot(sel_lin[...], recv_r[...].reshape(groups * lin_rows, LANES))
    hidden = []
    for i in range(steps):
        over_heads = []
        for h in range(heads):
            lanes = slice(h * LANES, (h + 1) * LANES)
            rows = slice((h * steps + i) * held, (h * steps + i + 1) * held)
            over_heads.append(gamma[i, :, lanes] * carried[rows] + own[i, :, lanes])
        hidden.append(jnp.concatenate(over_heads, axis=1))
    hidden = jnp.concatenate(hidden, axis=0).astype(BF16)
    by_distance = sorted(range(1, owners), key=lambda o: -min(o, owners - o))
    peers = [along_y(off) * 2 + core for off in by_distance for core in range(2)]
    peers.append(me_p + 1 - 2 * me_c)

    def sum_copy(part, peer):
        return pltpu.make_async_remote_copy(
            src_ref=part_b.at[part, peer],
            dst_ref=recv_p.at[part, me_p],
            send_sem=rs_send.at[part, peer],
            recv_sem=rs_recv.at[part, me_p],
            device_id=(me_s, me_r, peer),
            device_id_type=MESH,
        )

    for part in range(PARTS):
        for b in range(blocks_of):
            start = b * wide + part * narrow
            partial = dot(hidden, w[:, start : start + narrow])
            for i in range(steps):
                for core in range(2):
                    row = b * owned + (i % per_owner) * mine_each
                    here = i * held + core * mine_each
                    part_f[part, i // per_owner * 2 + core, row : row + mine_each, :] = partial[
                        here : here + mine_each
                    ]
        part_b[part] = part_f[part].astype(BF16)
        for peer in peers:
            sum_copy(part, peer).start()

    loads["ck"].wait()
    loads["cv"].wait()
    all_bytes(recv_b, b_sem.at[1])
    scale = LOG2E / math.sqrt(LANES)

    def soft(k):
        section = lax.div(dg_s[first + k], reps)
        place_of = jnp.int32(0)
        for k2 in range(held):
            same = (lax.div(dg_s[first + k2], reps) == section) & (k2 < k)
            place_of = place_of + jnp.where(same, 1, 0)
        block = recv_b[section, jnp.minimum(place_of, each - 1)]
        asked = block[:soft_rows]
        fresh_rows = block[soft_rows:]
        scores = dot_nt(asked, ck[k]) * scale
        scores = jnp.where(iota(scores.shape, 1) < len_s[first + k], scores, -jnp.inf)
        news = dot_nt(asked, fresh_rows) * scale
        lane = iota(news.shape, 1)
        seen = (lane < steps) & (lane <= lax.rem(iota(news.shape, 0), steps))
        news = jnp.where(seen, news, -jnp.inf)
        peak = jnp.maximum(
            jnp.max(scores, axis=1, keepdims=True), jnp.max(news, axis=1, keepdims=True)
        )
        scores = jnp.exp2(scores - peak)
        news = jnp.exp2(news - peak)
        bottom = jnp.sum(scores, axis=1, keepdims=True) + jnp.sum(news, axis=1, keepdims=True)
        probs = (scores / bottom).astype(BF16)
        fresh_probs = (news / bottom).astype(BF16).astype(F32)
        fresh_values = fresh_rows.astype(F32)
        mixed = dot(probs, cv[k])
        for u in range(steps):
            mixed = mixed + fresh_probs[:, u : u + 1] * fresh_values[steps + u : steps + u + 1]
        return mixed.astype(BF16)

    def requests_for(r):
        found = jnp.int32(0)
        for k in range(held):
            found = jnp.where(target_rep[k] == r, k, found)
        return found

    def answer_copy(peer_s, peer_r):
        return pltpu.make_async_remote_copy(
            src_ref=send_t.at[peer_r],
            dst_ref=recv_t.at[me_g],
            send_sem=t_sem.at[0],
            recv_sem=t_sem.at[1],
            device_id=(peer_s, peer_r, me_p),
            device_id_type=MESH,
        )

    rep_steps = sorted(
        ((dz, dx) for dz in (0, sections) for dx in range(across)),
        key=lambda d: -hops(d[0], deep) - hops(d[1], across),
    )
    batch = held
    for start in range(0, held, batch):
        chosen = rep_steps[start : start + batch]
        targets = [rep_at[dz] + x_at[dx] for dz, dx in chosen]
        answers = [soft(requests_for(r)) for r in targets]
        for r, answer in zip(targets, answers):
            send_t[r] = answer
        for (dz, dx), r, answer in zip(chosen, targets, answers):
            for ds in range(sections):
                if dz or dx or ds:
                    answer_copy(lax.rem(me_s + ds, sections), r).start()
                else:
                    recv_t[me_g] = answer

    summed = []
    for part in range(PARTS):
        here = slice(part * narrow, (part + 1) * narrow)
        value = part_f[part, me_p] + base_of[:, here]
        for source in reversed(peers):
            block = recv_p.at[part, source]
            pltpu.make_async_copy(block, block, rs_recv.at[part, source]).wait()
            value = value + recv_p[part, source].astype(F32)
        summed.append(value)
    square = jnp.sum(sum(value * value for value in summed), axis=1, keepdims=True)
    square = jnp.broadcast_to(square, (TILE, LANES))
    shift = TILE // 2
    while shift >= owned:
        square = square + pltpu.roll(square, shift, 0)
        shift //= 2
    spread_of = jnp.sqrt(square[:, :1] / model + 1e-06)

    def gather_copy(off):
        peer = along_y(off) * 2 + me_c
        return pltpu.make_async_remote_copy(
            src_ref=rows_of.at[me_p],
            dst_ref=rows_of.at[me_p],
            send_sem=ag_send.at[peer],
            recv_sem=ag_recv.at[me_p],
            device_id=(me_s, me_r, peer),
            device_id_type=MESH,
        )

    def pass_copy(y):
        source = y * 2 + me_c
        return pltpu.make_async_remote_copy(
            src_ref=rows_of.at[source],
            dst_ref=rows_of.at[source],
            send_sem=pass_send.at[y],
            recv_sem=ag_recv.at[source],
            device_id=sibling,
            device_id_type=MESH,
        )

    def landed(source):
        block = rows_of.at[source]
        pltpu.make_async_copy(block, block, ag_recv.at[source]).wait()

    for part in range(PARTS):
        here = slice(part * narrow, (part + 1) * narrow)
        rows_of[me_p, part] = (summed[part] / spread_of * gain_of[:, here]).astype(BF16)
    for off in by_distance:
        gather_copy(off).start()
    pass_copy(me_y).start()

    lax.fori_loop(early, held, prompt, 0)

    for off in reversed(by_distance):
        landed(along_y(off) * 2 + me_c)
        pass_copy(along_y(off)).start()

    all_bytes(recv_t, t_sem.at[1])
    placed = dot(sel_soft[...], recv_t[...].reshape(groups * soft_rows, LANES))
    for a in range(q_heads):
        for i in range(steps):
            rows = slice((a * steps + i) * held, (a * steps + i + 1) * held)
            so[i, :, a * LANES : (a + 1) * LANES] = placed[rows].astype(BF16)

    all_bytes(recv_q, q_sem.at[0])
    all_bytes(recv_r, r_sem.at[0])
    all_bytes(recv_a, a_sem.at[0])
    all_bytes(recv_b, b_sem.at[0])
    all_bytes(recv_t, t_sem.at[0])
    for part in range(PARTS):
        for peer in peers:
            sum_copy(part, peer).wait_send()

    shape = (blocks_of * per_owner * held, 2 * TILE)
    slot = lax.rem(iota(shape, 0), held)
    step = lax.rem(iota(shape, 0) // held, per_owner)
    block = iota(shape, 0) // (held * per_owner)
    wanted = (slot // mine_each) * TILE + block * owned + step * mine_each
    unpack = one_hot(wanted + lax.rem(slot, mine_each) == iota(shape, 1))
    for off in [0] + list(reversed(by_distance)):
        y = along_y(off)
        landed(y * 2 + 1 - me_c)
        for part in range(PARTS):
            pair = rows_of[pl.ds(y * 2, 2), part].reshape(2 * TILE, narrow)
            ordered = dot(unpack, pair)
            for b in range(blocks_of):
                start = b * wide + part * narrow
                for n in range(per_owner):
                    rows = slice((b * per_owner + n) * held, (b * per_owner + n + 1) * held)
                    do[y * per_owner + n, :, start : start + narrow] = ordered[rows].astype(BF16)
    for off in by_distance:
        gather_copy(off).wait_send()
    for y in range(owners):
        pass_copy(along_y(y)).wait_send()


def write_out(po, do, so, po_hbm, do_hbm, so_hbm, sem):
    held = po.shape[0]
    copies = [pltpu.make_async_copy(po.at[k], po_hbm.at[k], sem.at[k]) for k in range(held)]
    copies.append(pltpu.make_async_copy(do, do_hbm, sem.at[held]))
    copies.append(pltpu.make_async_copy(so, so_hbm, sem.at[held + 1]))
    for copy in copies:
        copy.start()
    for copy in copies:
        copy.wait()


def on_device(
    prefill_query,
    prefill_key,
    prefill_value,
    prefill_gate,
    lengths,
    decode_group,
    cache_keys,
    cache_values,
    out_weight,
    norm_gain,
    step_input,
    step_query,
    step_key,
    step_value,
    step_gate,
    soft_query,
    soft_new_key,
    soft_new_value,
):
    sections, reps, tps = (lax.axis_size(name) for name in ("section", "rep", "tp"))
    held, length, heads = prefill_gate.shape
    steps = step_query.shape[0]
    q_heads = soft_query.shape[2] // LANES
    model = out_weight.shape[1]
    groups = sections * reps
    width = heads * LANES
    per_owner = steps * 2 // tps
    narrow = model * per_owner * (held // 2) // TILE // PARTS
    lin_rows = heads * steps
    soft_rows = q_heads * steps
    total = groups * held
    dims = (sections, reps, tps, held, length, heads, steps, q_heads, model)
    operands = (
        prefill_query,
        prefill_key,
        prefill_value,
        jnp.transpose(prefill_gate, (0, 2, 1)),
        lengths,
        decode_group,
        decode_group.reshape(1, total),
        cache_keys,
        cache_values,
        out_weight,
        norm_gain.reshape(1, model),
        step_input,
        step_query,
        step_key,
        step_value,
        jnp.transpose(step_gate, (0, 2, 1)),
        soft_query,
        soft_new_key,
        soft_new_value,
    )
    vmem = pltpu.VMEM
    dma = pltpu.SemaphoreType.DMA
    scratch = [
        vmem((held, length, width), BF16),
        vmem((held, length, width), BF16),
        vmem((held, length, width), BF16),
        vmem((held, heads, length), F32),
        pltpu.SMEM((total,), jnp.int32),
        pltpu.SMEM((total,), jnp.int32),
        vmem((1, total), jnp.int32),
        vmem((held, length, LANES), BF16),
        vmem((held, length, LANES), BF16),
        vmem((width, model), BF16),
        vmem((1, model), F32),
        vmem((per_owner, held, model), BF16),
        vmem((steps, held, width), BF16),
        vmem((steps, held, width), BF16),
        vmem((steps, held, width), BF16),
        vmem((steps, heads, held), F32),
        vmem((steps, held, q_heads * LANES), BF16),
        vmem((steps, held, LANES), BF16),
        vmem((steps, held, LANES), BF16),
        vmem((held, heads, length), F32),
        vmem((held, length, heads), F32),
        vmem((held, length, heads), F32),
        vmem((held, heads, 2 * LANES, LANES), BF16),
        vmem((steps, held, width), F32),
        vmem((steps, held, width), F32),
        vmem((lin_rows * held, lin_rows * groups), BF16),
        vmem((soft_rows * held, soft_rows * groups), BF16),
        vmem((reps, lin_rows, LANES), BF16),
        vmem((groups, lin_rows, LANES), BF16),
        vmem((held, lin_rows, LANES), BF16),
        vmem((reps, lin_rows, LANES), BF16),
        vmem((groups, lin_rows, LANES), BF16),
        vmem((reps, soft_rows + lin_rows, LANES), BF16),
        vmem((reps, soft_rows + lin_rows, LANES), BF16),
        vmem((sections, held // sections, soft_rows + lin_rows, LANES), BF16),
        vmem((sections, held // sections, soft_rows + lin_rows, LANES), BF16),
        vmem((reps, soft_rows, LANES), BF16),
        vmem((groups, soft_rows, LANES), BF16),
        vmem((PARTS, tps, TILE, narrow), F32),
        vmem((PARTS, tps, TILE, narrow), BF16),
        vmem((PARTS, tps, TILE, narrow), BF16),
        vmem((TILE, PARTS * narrow), F32),
        vmem((TILE, PARTS * narrow), F32),
        vmem((tps, PARTS, TILE, narrow), BF16),
        dma((19,)),
        dma((2,)),
        dma((2,)),
        dma((2,)),
        dma((2,)),
        dma((2,)),
        dma((PARTS, tps)),
        dma((PARTS, tps)),
        dma((tps,)),
        dma((tps,)),
        dma((tps // 2,)),
    ]
    anywhere = pl.BlockSpec(memory_space=pl.ANY)
    results = pl.pallas_call(
        functools.partial(body, dims),
        out_shape=(
            vmem((held, length, width), BF16),
            vmem((steps, held, model), BF16),
            vmem((steps, held, q_heads * LANES), BF16),
        ),
        in_specs=[anywhere] * len(operands),
        out_specs=(pl.BlockSpec(memory_space=vmem),) * 3,
        scratch_shapes=scratch,
        compiler_params=pltpu.CompilerParams(
            collective_id=0, has_side_effects=True, vmem_limit_bytes=56 * 1024 * 1024
        ),
    )(*operands)
    results = [pltpu.with_memory_space_constraint(x, pltpu.VMEM) for x in results]
    return pl.pallas_call(
        write_out,
        out_shape=[jax.ShapeDtypeStruct(array.shape, array.dtype) for array in results],
        in_specs=[anywhere] * 3,
        out_specs=[anywhere] * 3,
        scratch_shapes=[dma((held + 2,))],
    )(*results)


def solution(mesh):
    rows = P(("section", "rep"), None, "tp")
    slots = P(None, ("section", "rep"), "tp")
    whole = P(None, ("section", "rep"), None)
    return jax.shard_map(
        on_device,
        mesh=mesh,
        in_specs=(
            rows,
            rows,
            rows,
            rows,
            P(),
            P(),
            rows,
            rows,
            P("tp", None),
            P(),
            whole,
            slots,
            slots,
            slots,
            slots,
            slots,
            slots,
            slots,
        ),
        out_specs=(rows, whole, slots),
        check_vma=False,
    )
```
